32 devices in a mesh: head: 2 (over core), blk: 16 (over z, y, x).
Axes of the slice: x: 2, y: 2, z: 4, core: 2. Of those that a mesh axis runs over, the one named last changes fastest.
Arguments:
- doc_x: bfloat16 [8192, 1024], P('blk'), may hold values from -27 to 27
- doc_query: bfloat16 [8192, 1024], P('blk', 'head'), may hold values from -36 to 36
- doc_key: bfloat16 [8192, 1024], P('blk', 'head'), may hold values from -36 to 36
- doc_value: bfloat16 [8192, 1024], P('blk', 'head'), may hold values from -8 to 8
- key_cache: bfloat16 [256, 16, 1024], P('blk', None, 'head'), may hold values from -9 to 9
- value_cache: bfloat16 [256, 16, 1024], P('blk', None, 'head'), may hold values from -8 to 8
- rel_embed: bfloat16 [512, 1024], replicated, may hold values from -6 to 6
- w_query: bfloat16 [1024, 1024], P(None, 'head'), may hold values from -0.1875 to 0.1875
- w_key: bfloat16 [1024, 1024], P(None, 'head'), may hold values from -0.1875 to 0.1875
- out_weight: bfloat16 [1024, 1024], P('head'), may hold values from -0.1875 to 0.1875
- ln_gain: float32 [1024], replicated, may hold values from 0.5 to 1.5
- ln_bias: float32 [1024], replicated, may hold values from -3 to 3
- score_weight: float32 [1024], replicated, may hold values from -0.1875 to 0.1875
- query_len: int32 [4], replicated, may hold values from 1 to 1024, as said below
- dev_query: int32 [16], replicated, may hold values from 0 to 3, as said below
- page_table: int32 [4, 64], replicated, may hold values from 0 to 255, as said below
- tile_kind: int32 [32], P('blk'), may hold values 0 or 1
- rel_bucket: int32 [511], replicated, may hold values from 1 to 511, as said below
Outputs:
- normed: bfloat16 [8192, 1024], P('blk', 'head')
- segment_scores: float32 [512], P('blk')
The draws below stay inside these ranges and needn't reach their ends.
Inputs may be any that keep to these rules, and one draw needn't show every extreme that they name: `query_len`: one query has exactly 1024 tokens. `dev_query`: each query is named by exactly 4 entries. `page_table`: a permutation of the 256 cache pages; the pages of one index of blk belong to 4 different queries, 4 page each. `rel_bucket`: entry 255 + d is the bucket of distance d; nondecreasing in d; 256 at d = 0; d = 1 and d = 2 share the next bucket above, d = -1 and d = -2 the next below.
All inputs are finite; a program needn't handle non-finite values. No bound on the sum of `tile_kind` on one device may be relied on, other than what follows from the above.
Results may differ from the reference program's by a relative error of at most 0.0075.
Values may be sent and summed in bfloat16 or wider, within the bound.
A program may use at most 192 MiB of HBM per device.

```python
import math
import jax
import jax.numpy as jnp
from jax import lax

D = 1024
HEADS = 16
HD = 64
BUCKETS = 512
DOCLEN = 256
SHORT = 16
QMAX = 1024
PAGE = 16
GROUP = 4
ROWS_DEV = 512
PAGES_DEV = 16
QPAGES = 64
QUERIES = 4
PAGES = 256
PMOST = 4
ROWS = 8192
TILES = 32
N_HEAD = 2


def draw_doc_x(key, part):
    base_key = jax.random.fold_in(key, 61)
    sample = jnp.clip(jax.random.normal(jax.random.fold_in(base_key, 1), (ROWS, D), jnp.float32), -4.0, 4.0)
    row_scale = jnp.exp(jax.random.uniform(jax.random.fold_in(base_key, 2), (ROWS, 1), jnp.float32, 0.0, math.log(3.2)))
    col_scale = jnp.exp(jax.random.uniform(jax.random.fold_in(base_key, 3), (1, D), jnp.float32, 0.0, math.log(3.2)))
    col_scale = col_scale * (1.0 + 2.0 * jnp.arange(D, dtype=jnp.float32)[None, :] / D)
    return (0.1 * sample * row_scale * col_scale).astype(jnp.bfloat16)


def draw_doc_query(key, part):
    sample = 1.5 * jnp.clip(jax.random.normal(jax.random.fold_in(key, 52), (ROWS, D), jnp.float32), -4.0, 4.0)
    return sample.astype(jnp.bfloat16)


def draw_doc_key(key, part):
    sample = 1.5 * jnp.clip(jax.random.normal(jax.random.fold_in(key, 53), (ROWS, D), jnp.float32), -4.0, 4.0)
    return sample.astype(jnp.bfloat16)


def draw_query_len(key, part):
    lengths = jax.random.randint(jax.random.fold_in(key, 22), (QUERIES,), 1, QMAX + 1)
    longest = jax.random.randint(jax.random.fold_in(key, 23), (), 0, QUERIES)
    lengths = jnp.where(jnp.arange(QUERIES) == longest, QMAX, lengths)
    return lengths.astype(jnp.int32)


def draw_dev_query(key, part):
    owners = jnp.arange(QUERIES * GROUP, dtype=jnp.int32) // GROUP
    return jax.random.permutation(jax.random.fold_in(key, 21), owners).astype(jnp.int32)


def draw_page_table(key, part):
    base_key = jax.random.fold_in(key, 31)
    blocks = PAGES // PAGES_DEV
    position = jnp.arange(PAGES, dtype=jnp.int32)
    labels = position // PMOST % QUERIES
    relabel = jax.random.permutation(jax.random.fold_in(base_key, 1), QUERIES)
    labels = relabel[labels].reshape(blocks, PAGES_DEV)
    order = jax.random.permutation(jax.random.fold_in(base_key, 2), blocks)
    labels = labels[order]
    within = jax.vmap(lambda row_key: jax.random.permutation(row_key, PAGES_DEV))(jax.random.split(jax.random.fold_in(base_key, 3), blocks))
    labels = jnp.take_along_axis(labels, within, axis=1).reshape(-1)
    jitter = jax.random.permutation(jax.random.fold_in(base_key, 4), PAGES)
    sorted_pages = jnp.argsort(labels * PAGES + jitter, stable=True)
    return sorted_pages.reshape(QUERIES, QPAGES).astype(jnp.int32)


def draw_rel_bucket(key, part):
    base_key = jax.random.fold_in(key, 41)
    upper_steps = jax.random.randint(jax.random.fold_in(base_key, 1), (DOCLEN - 1,), 0, 2)
    lower_steps = jax.random.randint(jax.random.fold_in(base_key, 2), (DOCLEN - 1,), 0, 2)
    step_ids = jnp.arange(DOCLEN - 1)
    upper_steps = jnp.where(step_ids == 0, 1, jnp.where(step_ids == 1, 0, upper_steps))
    lower_steps = jnp.where(step_ids == 0, 1, jnp.where(step_ids == 1, 0, lower_steps))
    upper = jnp.cumsum(upper_steps)
    lower = jnp.cumsum(lower_steps)
    upper = jnp.where(step_ids == DOCLEN - 2, DOCLEN - 1, upper)
    lower = jnp.where(step_ids == DOCLEN - 2, DOCLEN - 1, lower)
    centre = BUCKETS // 2
    middle = jnp.full((1,), centre, jnp.int32)
    return jnp.concatenate([centre - lower[::-1], middle, centre + upper]).astype(jnp.int32)


def with_ends(result, own_key, smallest, high):
    longest = result.shape.index(max(result.shape))
    spots = []
    for shift in (0, 1):
        where = [jax.random.randint(jax.random.fold_in(own_key, axis), (), 0, length) for axis, length in enumerate(result.shape)]
        where[longest] = (where[longest] + shift) % result.shape[longest]
        spots.append(tuple(where))
    return result.at[spots[0]].set(smallest).at[spots[1]].set(high)


def block_levels(rng, extent, pieces, low, largest):
    factor_of, own = 1.0, jax.random.fold_in(rng, 6)
    for dim, blocks in pieces:
        heights = jnp.exp(jax.random.uniform(jax.random.fold_in(own, dim), (blocks,), jnp.float32, low / len(pieces), largest / len(pieces)))
        factor_of = factor_of * jnp.repeat(heights, extent[dim] // blocks).reshape([-1 if axis == dim else 1 for axis in range(len(extent))])
    return factor_of


def scatter_about(rng, dims, deviation, limit, pieces=(), kind=jnp.bfloat16):
    level = block_levels(rng, dims, pieces, -0.22, 0.18) if pieces else 1.0
    drawn = jax.random.normal(rng, dims, jnp.float32) * deviation * level
    return jnp.minimum(jnp.maximum(drawn, -limit), limit).astype(kind)


def setup_inputs(seed: int = 0) -> dict:
    streams_of = jax.random.split(jax.random.key(seed), 19)
    return {
        "doc_x": draw_doc_x(jax.random.fold_in(streams_of[18], 71), 0),
        "doc_query": draw_doc_query(jax.random.fold_in(streams_of[18], 71), 0),
        "doc_key": draw_doc_key(jax.random.fold_in(streams_of[18], 71), 0),
        "doc_value": scatter_about(streams_of[3], (ROWS, D), 2.0, 8.0, ((0, 16), (1, 2))),
        "key_cache": scatter_about(streams_of[4], (PAGES, PAGE, D), 1.5, 9.0, ((0, 16), (2, 2))),
        "value_cache": scatter_about(streams_of[5], (PAGES, PAGE, D), 2.0, 8.0, ((0, 16), (2, 2))),
        "rel_embed": scatter_about(streams_of[6], (BUCKETS, D), 1.0, 6.0),
        "w_query": scatter_about(streams_of[7], (D, D), D ** -0.5, 0.1875, ((1, 2),)),
        "w_key": scatter_about(streams_of[8], (D, D), D ** -0.5, 0.1875, ((1, 2),)),
        "out_weight": scatter_about(streams_of[9], (D, D), D ** -0.5, 0.1875, ((0, 2),)),
        "ln_gain": jnp.clip(1.0 + 0.1 * jax.random.normal(streams_of[10], (D,), jnp.float32), 0.5, 1.5),
        "ln_bias": scatter_about(streams_of[11], (D,), 0.5, 3.0, (), jnp.float32),
        "score_weight": scatter_about(streams_of[12], (D,), D ** -0.5, 0.1875, (), jnp.float32),
        "query_len": draw_query_len(jax.random.fold_in(streams_of[18], 71), 0),
        "dev_query": draw_dev_query(jax.random.fold_in(streams_of[18], 71), 0),
        "page_table": draw_page_table(jax.random.fold_in(streams_of[18], 71), 0),
        "tile_kind": with_ends((jax.random.randint(streams_of[16], (TILES,), 0, 2) < 1).astype(jnp.int32), jax.random.fold_in(streams_of[16], 1), 0, 1),
        "rel_bucket": draw_rel_bucket(jax.random.fold_in(streams_of[18], 71), 0),
    }


def reference(doc_x, doc_query, doc_key, doc_value, key_cache, value_cache, rel_embed, w_query, w_key, out_weight, ln_gain, ln_bias, score_weight, query_len, dev_query, page_table, tile_kind, rel_bucket):
    scaling = 1.0 / (3.0 * HD) ** 0.5
    pos_key = jnp.dot(rel_embed, w_key, preferred_element_type=jnp.float32).astype(jnp.bfloat16)
    pos_query = jnp.dot(rel_embed, w_query, preferred_element_type=jnp.float32).astype(jnp.bfloat16)
    key_rel = pos_key[rel_bucket].reshape(2 * DOCLEN - 1, HEADS, HD).astype(jnp.float32)
    query_rel = pos_query[rel_bucket].reshape(2 * DOCLEN - 1, HEADS, HD).astype(jnp.float32)
    places = jnp.arange(DOCLEN, dtype=jnp.int32)
    shift_index = places[:, None] - places[None, :] + DOCLEN - 1
    shift_index = jnp.broadcast_to(shift_index[None], (HEADS, DOCLEN, DOCLEN))
    same_short = places[:, None] // SHORT == places[None, :] // SHORT
    tokens_pos = jnp.arange(QMAX, dtype=jnp.int32)
    tiles_dev = ROWS_DEV // DOCLEN

    def one_tile(tile_id):
        query_id = dev_query[tile_id // tiles_dev]
        page_rows = page_table[query_id]
        cache_keys = key_cache[page_rows].reshape(QMAX, HEADS, HD).astype(jnp.float32)
        cache_values = value_cache[page_rows].reshape(QMAX, HEADS, HD).astype(jnp.float32)
        valid_keys = tokens_pos < query_len[query_id]
        row_start = (tile_id * DOCLEN).astype(jnp.int32)
        tile_query = lax.dynamic_slice_in_dim(doc_query, row_start, DOCLEN, 0).reshape(DOCLEN, HEADS, HD).astype(jnp.float32)
        tile_key = lax.dynamic_slice_in_dim(doc_key, row_start, DOCLEN, 0).reshape(DOCLEN, HEADS, HD).astype(jnp.float32)
        tile_value = lax.dynamic_slice_in_dim(doc_value, row_start, DOCLEN, 0).reshape(DOCLEN, HEADS, HD).astype(jnp.float32)
        cross_part = jnp.einsum('ihd,thd->hit', tile_query, cache_keys) * scaling
        cross_part = jnp.where(valid_keys[None, None, :], cross_part, -jnp.inf)
        content = jnp.einsum('ihd,jhd->hij', tile_query, tile_key)
        c2p_all = jnp.einsum('ihd,rhd->hir', tile_query, key_rel)
        c2p_part = jnp.take_along_axis(c2p_all, shift_index, axis=2)
        p2c_all = jnp.einsum('jhd,rhd->hjr', tile_key, query_rel)
        p2c_part = jnp.swapaxes(jnp.take_along_axis(p2c_all, shift_index, axis=2), 1, 2)
        own_part = (content + c2p_part + p2c_part) * scaling
        allowed = jnp.logical_or(tile_kind[tile_id] == 1, same_short)
        own_part = jnp.where(allowed[None], own_part, -jnp.inf)
        scores = jnp.concatenate([cross_part, own_part], axis=2)
        row_top = lax.optimization_barrier(jnp.max(scores, axis=2, keepdims=True))
        expo_terms = jnp.exp(scores - row_top)
        weights = (expo_terms / lax.optimization_barrier(jnp.sum(expo_terms, axis=2, keepdims=True))).astype(jnp.bfloat16)
        wide_weights = weights.astype(jnp.float32)
        attended = jnp.einsum('hit,thd->ihd', wide_weights[:, :, :QMAX], cache_values)
        attended = attended + jnp.einsum('hij,jhd->ihd', wide_weights[:, :, QMAX:], tile_value)
        return attended.reshape(DOCLEN, D).astype(jnp.bfloat16)
    attended = lax.map(one_tile, jnp.arange(TILES, dtype=jnp.int32)).reshape(ROWS, D)
    group_cols = D // N_HEAD
    hidden = doc_x.astype(jnp.float32)
    for group_id in range(N_HEAD):
        partial_value = jnp.dot(attended[:, group_id * group_cols:(group_id + 1) * group_cols], out_weight[group_id * group_cols:(group_id + 1) * group_cols], preferred_element_type=jnp.float32).astype(jnp.bfloat16)
        partial_value = lax.optimization_barrier(partial_value)
        hidden = hidden + partial_value.astype(jnp.float32)
    row_mean = lax.optimization_barrier(jnp.mean(hidden, axis=1, keepdims=True))
    centred = hidden - row_mean
    variance = lax.optimization_barrier(jnp.mean(centred * centred, axis=1, keepdims=True))
    normed_full = centred * lax.rsqrt(variance + 1e-07) * ln_gain[None, :] + ln_bias[None, :]
    segment_scores = lax.optimization_barrier(jnp.sum(normed_full[::SHORT] * score_weight[None, :], axis=1))
    return (normed_full.astype(jnp.bfloat16), segment_scores)
```

```python
import functools

import jax
import jax.numpy as jnp
from jax import lax
from jax.experimental import pallas as pl
from jax.experimental.pallas import tpu as pltpu
from jax.sharding import PartitionSpec as P

HD = 64
DOCLEN = 256
SHORT = 16
MESH = pl.DeviceIdType.MESH
F32 = jnp.float32
BF16 = jnp.bfloat16
NEG = float("-inf")


def dot_t(a, b):
    return lax.dot_general(a, b, (((1,), (1,)), ((), ())), preferred_element_type=F32)


def skew(table):
    return pltpu.roll(table, 0, 1, stride=1, stride_axis=0)[:, DOCLEN:]


def kernel(
    n,
    slots,
    index_ref,
    kind_ref,
    keyc_ref,
    valuec_ref,
    embed_ref,
    wk_ref,
    wq_ref,
    bucket_ref,
    bias_ref,
    q_ref,
    k_ref,
    v_ref,
    ow_ref,
    x_ref,
    gain_ref,
    lnb_ref,
    sw_ref,
    out_ref,
    seg_ref,
    send_k,
    send_v,
    recv_k,
    recv_v,
    key_rel,
    query_rel,
    own,
    probs,
    att,
    part,
    other,
    hidden,
    send_sem,
    recv_sem,
    pair_send,
    pair_recv,
):
    me = lax.axis_index("blk")
    head = lax.axis_index("head")
    page = keyc_ref.shape[1]
    block = slots * page
    rows, cols = q_ref.shape
    tiles = rows // DOCLEN
    pairs = cols // (2 * HD)
    model = x_ref.shape[1]
    tokens = recv_k.shape[0]
    factor = float(1.4426950408889634 / (3.0 * HD) ** 0.5)

    barrier = pltpu.get_barrier_semaphore()

    def greet(step, carry):
        pl.semaphore_signal(
            barrier, inc=1, device_id={"blk": lax.rem(me + step, n)}, device_id_type=MESH
        )
        return carry

    lax.fori_loop(1, n, greet, 0)
    pl.semaphore_signal(barrier, inc=1, device_id={"head": 1 - head}, device_id_type=MESH)

    def pack(source, packed, dest):
        for slot in range(slots):
            packed[pl.ds(pl.multiple_of(dest * block + slot * page, page), page), :] = source[
                index_ref[dest * slots + slot]
            ]

    def pack_all(dest, carry):
        pack(keyc_ref, send_k, dest)
        pack(valuec_ref, send_v, dest)
        return carry

    lax.fori_loop(0, n, pack_all, 0)
    pl.semaphore_wait(barrier, n)

    def transfer(packed, landing, which, step):
        dest = lax.rem(me + step, n)
        return pltpu.make_async_remote_copy(
            src_ref=packed.at[pl.ds(pl.multiple_of(dest * block, block), block)],
            dst_ref=landing.at[pl.ds(pl.multiple_of(me * block, block), block)],
            send_sem=send_sem.at[which, step],
            recv_sem=recv_sem.at[which, step],
            device_id={"blk": dest},
            device_id_type=MESH,
        )

    def start_k(step, carry):
        transfer(send_k, recv_k, 0, step).start()
        return carry

    def start_v(step, carry):
        transfer(send_v, recv_v, 1, step).start()
        return carry

    lax.fori_loop(1, n, start_k, 0)
    lax.fori_loop(1, n, start_v, 0)
    mine = pl.ds(pl.multiple_of(me * block, block), block)
    recv_k[mine, :] = send_k[mine, :]
    recv_v[mine, :] = send_v[mine, :]

    picker = (
        bucket_ref[...] == lax.broadcasted_iota(jnp.int32, (2 * DOCLEN, embed_ref.shape[0]), 1)
    ).astype(BF16)
    for weight, table in ((wk_ref, key_rel), (wq_ref, query_rel)):
        projected = jnp.dot(embed_ref[...], weight[...], preferred_element_type=F32).astype(BF16)
        table[...] = jnp.dot(picker, projected, preferred_element_type=F32).astype(BF16)

    lane = lax.broadcasted_iota(jnp.int32, (1, 2 * HD), 1)
    halves = (lane < HD, lane >= HD)
    same_short = (
        lax.broadcasted_iota(jnp.int32, (DOCLEN, DOCLEN), 0) // SHORT
        == lax.broadcasted_iota(jnp.int32, (DOCLEN, DOCLEN), 1) // SHORT
    )

    def place(step):
        tile, pair = step // pairs, step % pairs
        tile_rows = pl.ds(pl.multiple_of(tile * DOCLEN, DOCLEN), DOCLEN)
        pair_cols = pl.ds(pl.multiple_of(pair * 2 * HD, 2 * HD), 2 * HD)
        return tile, tile_rows, pair_cols

    def own_scores(step, carry):
        tile, tile_rows, pair_cols = place(step)
        q = q_ref[tile_rows, pair_cols]
        k = k_ref[tile_rows, pair_cols]
        kr = key_rel[:, pair_cols]
        qr = query_rel[:, pair_cols]
        allowed = jnp.where(same_short, 1, kind_ref[tile]) == 1
        for half in range(2):
            qh = jnp.where(halves[half], q, jnp.zeros_like(q))
            kh = jnp.where(halves[half], k, jnp.zeros_like(k))
            scores = dot_t(qh, k) + skew(dot_t(qh, kr)) + skew(dot_t(kh, qr)).T
            own[step * 2 + half] = jnp.where(allowed, scores, NEG)
        return carry

    lax.fori_loop(0, tiles * pairs, own_scores, 0)

    def land_k(step, carry):
        transfer(send_k, recv_k, 0, step).wait_recv()
        return carry

    lax.fori_loop(1, n, land_k, 0)

    def weigh(step, carry):
        tile, tile_rows, pair_cols = place(step)
        q = q_ref[tile_rows, pair_cols]
        keys = recv_k[:, pair_cols]
        for half in range(2):
            qh = jnp.where(halves[half], q, jnp.zeros_like(q))
            cross = dot_t(qh, keys) + bias_ref[...]
            inner = own[step * 2 + half]
            top = jnp.maximum(
                jnp.max(cross, axis=1, keepdims=True), jnp.max(inner, axis=1, keepdims=True)
            )
            probs[step * 2 + half, :, :tokens] = jnp.exp2((cross - top) * factor).astype(BF16)
            probs[step * 2 + half, :, tokens:] = jnp.exp2((inner - top) * factor).astype(BF16)
        return carry

    lax.fori_loop(0, tiles * pairs, weigh, 0)

    def land_v(step, carry):
        transfer(send_v, recv_v, 1, step).wait_recv()
        return carry

    lax.fori_loop(1, n, land_v, 0)

    def gather_values(step, carry):
        tile, tile_rows, pair_cols = place(step)
        values = recv_v[:, pair_cols]
        inner = v_ref[tile_rows, pair_cols]
        sums = []
        for half in range(2):
            weights = probs[step * 2 + half]
            sums.append(
                jnp.dot(
                    weights[:, :tokens],
                    jnp.where(halves[half], values, jnp.ones_like(values)),
                    preferred_element_type=F32,
                )
                + jnp.dot(
                    weights[:, tokens:],
                    jnp.where(halves[half], inner, jnp.ones_like(inner)),
                    preferred_element_type=F32,
                )
            )
        top = jnp.where(halves[0], sums[0], sums[1])
        below = pltpu.roll(jnp.where(halves[0], sums[1], sums[0]), HD, 1)
        att[tile_rows, pair_cols] = (top / below).astype(BF16)
        return carry

    def swap(tile):
        return pltpu.make_async_remote_copy(
            src_ref=part.at[tile],
            dst_ref=other.at[tile],
            send_sem=pair_send.at[tile],
            recv_sem=pair_recv.at[tile],
            device_id={"head": 1 - head},
            device_id_type=MESH,
        )

    for tile in range(tiles):
        lax.fori_loop(tile * pairs, (tile + 1) * pairs, gather_values, 0)
        part[tile] = jnp.dot(
            att[tile * DOCLEN : (tile + 1) * DOCLEN, :], ow_ref[...], preferred_element_type=F32
        ).astype(BF16)
        swap(tile).start()

    here = pl.ds(pl.multiple_of(head * (model // 2), model // 2), model // 2)
    for tile in range(tiles):
        span = slice(tile * DOCLEN, (tile + 1) * DOCLEN)
        swap(tile).wait_recv()
        total = (
            x_ref[span, :].astype(F32) + part[tile].astype(F32) + other[tile].astype(F32)
        )
        mean = jnp.mean(total, axis=1, keepdims=True)
        centred = total - mean
        spread = jnp.mean(centred * centred, axis=1, keepdims=True)
        hidden[...] = centred * lax.rsqrt(spread + 1e-07)
        out_ref[span, :] = (
            hidden[:, here] * gain_ref[:, here] + lnb_ref[:, here]
        ).astype(BF16)
        firsts = jnp.concatenate(
            [hidden[row : row + 1, :] for row in range(0, DOCLEN, SHORT)], axis=0
        )
        full = firsts * gain_ref[...] + lnb_ref[...]
        seg_ref[tile * (DOCLEN // SHORT) : (tile + 1) * (DOCLEN // SHORT), :] = jnp.sum(
            full * sw_ref[...], axis=1, keepdims=True
        )

    def drain(step, carry):
        transfer(send_k, recv_k, 0, step).wait_send()
        transfer(send_v, recv_v, 1, step).wait_send()
        return carry

    lax.fori_loop(1, n, drain, 0)
    for tile in range(tiles):
        swap(tile).wait_send()


def shards(
    n,
    doc_x,
    doc_query,
    doc_key,
    doc_value,
    key_cache,
    value_cache,
    rel_embed,
    w_query,
    w_key,
    out_weight,
    ln_gain,
    ln_bias,
    score_weight,
    query_len,
    dev_query,
    page_table,
    tile_kind,
    rel_bucket,
):
    pages_here, page, cols = key_cache.shape
    queries, query_pages = page_table.shape
    slots = pages_here // queries
    tokens = query_pages * page
    rows, model = doc_x.shape
    tiles = rows // DOCLEN
    heads_here = cols // HD
    me = lax.axis_index("blk")

    rank = jnp.sum(
        (page_table[:, None, :] < page_table[:, :, None]).astype(jnp.int32), axis=2
    )
    wanted_rank = me * slots + jnp.arange(slots, dtype=jnp.int32)
    local = jnp.sum(
        jnp.where(rank[:, None, :] == wanted_rank[None, :, None], page_table[:, None, :], 0),
        axis=2,
    ) - me * pages_here
    names = dev_query[:, None] == jnp.arange(queries, dtype=jnp.int32)[None, :]
    index = jnp.sum(jnp.where(names[:, :, None], local[None], 0), axis=1).reshape(-1)
    my_query = dev_query[me]
    my_rank = rank[my_query]
    order = jnp.arange(query_pages, dtype=jnp.int32)
    page_of = jnp.sum(jnp.where(my_rank[None, :] == order[:, None], order[None, :], 0), axis=1)
    token = page_of[:, None] * page + jnp.arange(page, dtype=jnp.int32)[None, :]
    bias = jnp.where(token < query_len[my_query], 0.0, NEG).astype(F32).reshape(1, tokens)
    bucket = jnp.concatenate([jnp.full((1,), -1, jnp.int32), rel_bucket[::-1]])[:, None]

    vmem = pl.BlockSpec(memory_space=pltpu.VMEM)
    smem = pl.BlockSpec(memory_space=pltpu.SMEM)
    normed, seg = pl.pallas_call(
        functools.partial(kernel, n, slots),
        out_shape=(
            jax.ShapeDtypeStruct((rows, model // 2), BF16),
            jax.ShapeDtypeStruct((rows // SHORT, 1), F32),
        ),
        in_specs=[smem, smem] + [vmem] * 15,
        out_specs=(vmem, vmem),
        scratch_shapes=[
            pltpu.VMEM((n * slots * page, cols), BF16),
            pltpu.VMEM((n * slots * page, cols), BF16),
            pltpu.VMEM((tokens, cols), BF16),
            pltpu.VMEM((tokens, cols), BF16),
            pltpu.VMEM((2 * DOCLEN, cols), BF16),
            pltpu.VMEM((2 * DOCLEN, cols), BF16),
            pltpu.VMEM((tiles * heads_here, DOCLEN, DOCLEN), F32),
            pltpu.VMEM((tiles * heads_here, DOCLEN, tokens + DOCLEN), BF16),
            pltpu.VMEM((rows, cols), BF16),
            pltpu.VMEM((tiles, DOCLEN, model), BF16),
            pltpu.VMEM((tiles, DOCLEN, model), BF16),
            pltpu.VMEM((DOCLEN, model), F32),
            pltpu.SemaphoreType.DMA((2, n)),
            pltpu.SemaphoreType.DMA((2, n)),
            pltpu.SemaphoreType.DMA((tiles,)),
            pltpu.SemaphoreType.DMA((tiles,)),
        ],
        compiler_params=pltpu.CompilerParams(
            collective_id=0, has_side_effects=True, vmem_limit_bytes=56 * 1024 * 1024
        ),
        cost_estimate=pl.CostEstimate(
            flops=8_000_000_000, bytes_accessed=12_000_000, transcendentals=5_000_000
        ),
    )(
        index,
        tile_kind,
        key_cache,
        value_cache,
        rel_embed,
        w_key,
        w_query,
        bucket,
        bias,
        doc_query,
        doc_key,
        doc_value,
        out_weight,
        doc_x,
        ln_gain[None, :],
        ln_bias[None, :],
        score_weight[None, :],
    )
    return normed, seg.reshape(-1)


def solution(mesh):
    in_specs = (
        P("blk", None),
        P("blk", "head"),
        P("blk", "head"),
        P("blk", "head"),
        P("blk", None, "head"),
        P("blk", None, "head"),
        P(),
        P(None, "head"),
        P(None, "head"),
        P("head", None),
        P(),
        P(),
        P(),
        P(),
        P(),
        P(),
        P("blk"),
        P(),
    )
    out_specs = (P("blk", "head"), P("blk"))
    return jax.shard_map(
        functools.partial(shards, mesh.shape["blk"]),
        mesh=mesh,
        in_specs=in_specs,
        out_specs=out_specs,
        check_vma=False,
    )
```

```python
import functools

import jax
import jax.numpy as jnp
from jax import lax
from jax.experimental import pallas as pl
from jax.experimental.pallas import tpu as pltpu
from jax.sharding import PartitionSpec as P

HD = 64
DOCLEN = 256
SHORT = 16
MESH = pl.DeviceIdType.MESH
F32 = jnp.float32
BF16 = jnp.bfloat16
NEG = float("-inf")


def dot_t(a, b):
    return lax.dot_general(a, b, (((1,), (1,)), ((), ())), preferred_element_type=F32)


def skew(table):
    return pltpu.roll(table, 0, 1, stride=1, stride_axis=0)[:, DOCLEN:]


def kernel(
    n,
    kind_ref,
    asked_ref,
    length_ref,
    table_ref,
    keyc_ref,
    valuec_ref,
    bucket_ref,
    gain_ref,
    lnb_ref,
    sw_ref,
    embed_hbm,
    wk_hbm,
    wq_hbm,
    q_hbm,
    k_hbm,
    v_hbm,
    ow_hbm,
    x_hbm,
    out_ref,
    seg_ref,
    embed_ref,
    wk_ref,
    wq_ref,
    q_ref,
    k_ref,
    v_ref,
    ow_ref,
    x_ref,
    sorted_k,
    sorted_v,
    send_k,
    send_v,
    recv_k,
    recv_v,
    key_rel,
    query_rel,
    own,
    probs,
    att,
    part,
    other,
    hidden,
    load_sem,
    send_sem,
    recv_sem,
    pair_send,
    pair_recv,
):
    me = lax.axis_index("blk")
    head = lax.axis_index("head")
    pages_here, page, cols = keyc_ref.shape
    queries, query_pages = table_ref.shape
    block = pages_here // queries * page
    rows = q_ref.shape[0]
    tiles = rows // DOCLEN
    pairs = cols // (2 * HD)
    model = x_ref.shape[1]
    tokens = recv_k.shape[0]
    local = pages_here * page
    factor = float(1.4426950408889634 / (3.0 * HD) ** 0.5)

    barrier = pltpu.get_barrier_semaphore()

    def greet(step, carry):
        pl.semaphore_signal(
            barrier, inc=1, device_id={"blk": lax.rem(me + step, n)}, device_id_type=MESH
        )
        return carry

    lax.fori_loop(1, n, greet, 0)
    pl.semaphore_signal(barrier, inc=1, device_id={"head": 1 - head}, device_id_type=MESH)

    loads = [
        pltpu.make_async_copy(source, target, load_sem.at[place])
        for place, (source, target) in enumerate(
            (
                (embed_hbm, embed_ref),
                (wk_hbm, wk_ref),
                (wq_hbm, wq_ref),
                (q_hbm, q_ref),
                (k_hbm, k_ref),
                (v_hbm, v_ref),
                (ow_hbm, ow_ref),
                (x_hbm, x_ref),
            )
        )
    ]
    for load in loads:
        load.start()

    def iota(shape, axis):
        return lax.broadcasted_iota(jnp.int32, shape, axis)

    square = (query_pages, query_pages)
    diagonal = iota(square, 0) == iota(square, 1)

    def upright(line):
        return jnp.sum(jnp.where(diagonal, line, 0), axis=1, keepdims=True)

    token = iota((1, local), 1)
    first = me * pages_here
    page_id = first + token // page
    target = jnp.zeros((1, local), jnp.int32)
    for query in range(queries):
        listed = upright(table_ref[query : query + 1, :])
        hit = jnp.sum((listed == page_id).astype(jnp.int32), axis=0, keepdims=True)
        before = jnp.sum(
            jnp.logical_and(listed >= first, listed < page_id).astype(jnp.int32),
            axis=0,
            keepdims=True,
        )
        target = target + hit * (query * block + before * page)
    target = target + token % page
    order = (iota((local, local), 0) == target).astype(BF16)
    for source, arranged in ((keyc_ref, sorted_k), (valuec_ref, sorted_v)):
        arranged[...] = (
            jnp.dot(order, source[...].reshape(local, cols), preferred_element_type=F32)
            .astype(BF16)
            .reshape(queries, block, cols)
        )

    def pack(dest, carry):
        spot = pl.ds(pl.multiple_of(dest * block, block), block)
        send_k[spot, :] = sorted_k[asked_ref[dest]]
        send_v[spot, :] = sorted_v[asked_ref[dest]]
        return carry

    lax.fori_loop(0, n, pack, 0)
    pl.semaphore_wait(barrier, n)

    def transfer(packed, landing, which, step):
        dest = lax.rem(me + step, n)
        return pltpu.make_async_remote_copy(
            src_ref=packed.at[pl.ds(pl.multiple_of(dest * block, block), block)],
            dst_ref=landing.at[pl.ds(pl.multiple_of(me * block, block), block)],
            send_sem=send_sem.at[which, step],
            recv_sem=recv_sem.at[which, step],
            device_id={"blk": dest},
            device_id_type=MESH,
        )

    def start_k(step, carry):
        transfer(send_k, recv_k, 0, step).start()
        return carry

    def start_v(step, carry):
        transfer(send_v, recv_v, 1, step).start()
        return carry

    lax.fori_loop(1, n, start_k, 0)
    lax.fori_loop(1, n, start_v, 0)
    mine = pl.ds(pl.multiple_of(me * block, block), block)
    recv_k[mine, :] = send_k[mine, :]
    recv_v[mine, :] = send_v[mine, :]

    my_query = asked_ref[me]
    wanted = jnp.sum(
        jnp.where(iota((queries, query_pages), 0) == my_query, table_ref[...], 0),
        axis=0,
        keepdims=True,
    )
    rank = jnp.sum((wanted < upright(wanted)).astype(jnp.int32), axis=1, keepdims=True)
    spread_shape = (query_pages, tokens)
    place_id = jnp.sum(
        jnp.where(rank == iota(spread_shape, 1) // page, iota(spread_shape, 0), 0),
        axis=0,
        keepdims=True,
    )
    allowed_token = place_id * page + iota((1, tokens), 1) % page < length_ref[my_query]
    bias = jnp.where(allowed_token, 0.0, NEG).astype(F32)

    buckets = embed_ref.shape[0]
    distances = bucket_ref.shape[1]
    flipped = iota((2 * DOCLEN, distances), 0) + iota((2 * DOCLEN, distances), 1) == distances
    bucket = jnp.sum(jnp.where(flipped, bucket_ref[...], 0), axis=1, keepdims=True)
    for load in loads[:3]:
        load.wait()
    picker = (bucket == iota((2 * DOCLEN, buckets), 1)).astype(BF16)
    for weight, table in ((wk_ref, key_rel), (wq_ref, query_rel)):
        projected = jnp.dot(embed_ref[...], weight[...], preferred_element_type=F32).astype(BF16)
        table[...] = jnp.dot(picker, projected, preferred_element_type=F32).astype(BF16)

    lane = lax.broadcasted_iota(jnp.int32, (1, 2 * HD), 1)
    halves = (lane < HD, lane >= HD)
    same_short = (
        lax.broadcasted_iota(jnp.int32, (DOCLEN, DOCLEN), 0) // SHORT
        == lax.broadcasted_iota(jnp.int32, (DOCLEN, DOCLEN), 1) // SHORT
    )

    def place(step):
        tile, pair = step // pairs, step % pairs
        tile_rows = pl.ds(pl.multiple_of(tile * DOCLEN, DOCLEN), DOCLEN)
        pair_cols = pl.ds(pl.multiple_of(pair * 2 * HD, 2 * HD), 2 * HD)
        return tile, tile_rows, pair_cols

    def own_scores(step, carry):
        tile, tile_rows, pair_cols = place(step)
        q = q_ref[tile_rows, pair_cols]
        k = k_ref[tile_rows, pair_cols]
        kr = key_rel[:, pair_cols]
        qr = query_rel[:, pair_cols]
        allowed = jnp.where(same_short, 1, kind_ref[tile]) == 1
        for half in range(2):
            qh = jnp.where(halves[half], q, jnp.zeros_like(q))
            kh = jnp.where(halves[half], k, jnp.zeros_like(k))
            scores = dot_t(qh, k) + skew(dot_t(qh, kr)) + skew(dot_t(kh, qr)).T
            own[step * 2 + half] = jnp.where(allowed, scores, NEG)
        return carry

    for load in loads[3:]:
        load.wait()
    lax.fori_loop(0, tiles * pairs, own_scores, 0)

    def land_k(step, carry):
        transfer(send_k, recv_k, 0, step).wait_recv()
        return carry

    lax.fori_loop(1, n, land_k, 0)

    def weigh(step, carry):
        tile, tile_rows, pair_cols = place(step)
        q = q_ref[tile_rows, pair_cols]
        keys = recv_k[:, pair_cols]
        for half in range(2):
            qh = jnp.where(halves[half], q, jnp.zeros_like(q))
            cross = dot_t(qh, keys) + bias
            inner = own[step * 2 + half]
            top = jnp.maximum(
                jnp.max(cross, axis=1, keepdims=True), jnp.max(inner, axis=1, keepdims=True)
            )
            probs[step * 2 + half, :, :tokens] = jnp.exp2((cross - top) * factor).astype(BF16)
            probs[step * 2 + half, :, tokens:] = jnp.exp2((inner - top) * factor).astype(BF16)
        return carry

    lax.fori_loop(0, tiles * pairs, weigh, 0)

    def land_v(step, carry):
        transfer(send_v, recv_v, 1, step).wait_recv()
        return carry

    lax.fori_loop(1, n, land_v, 0)

    def gather_values(step, carry):
        tile, tile_rows, pair_cols = place(step)
        values = recv_v[:, pair_cols]
        inner = v_ref[tile_rows, pair_cols]
        sums = []
        for half in range(2):
            weights = probs[step * 2 + half]
            sums.append(
                jnp.dot(
                    weights[:, :tokens],
                    jnp.where(halves[half], values, jnp.ones_like(values)),
                    preferred_element_type=F32,
                )
                + jnp.dot(
                    weights[:, tokens:],
                    jnp.where(halves[half], inner, jnp.ones_like(inner)),
                    preferred_element_type=F32,
                )
            )
        top = jnp.where(halves[0], sums[0], sums[1])
        below = pltpu.roll(jnp.where(halves[0], sums[1], sums[0]), HD, 1)
        att[tile_rows, pair_cols] = (top / below).astype(BF16)
        return carry

    def swap(tile):
        return pltpu.make_async_remote_copy(
            src_ref=part.at[tile],
            dst_ref=other.at[tile],
            send_sem=pair_send.at[tile],
            recv_sem=pair_recv.at[tile],
            device_id={"head": 1 - head},
            device_id_type=MESH,
        )

    for tile in range(tiles):
        lax.fori_loop(tile * pairs, (tile + 1) * pairs, gather_values, 0)
        part[tile] = jnp.dot(
            att[tile * DOCLEN : (tile + 1) * DOCLEN, :], ow_ref[...], preferred_element_type=F32
        ).astype(BF16)
        swap(tile).start()

    seg_row = jnp.zeros(seg_ref.shape, F32)
    here = pl.ds(pl.multiple_of(head * (model // 2), model // 2), model // 2)
    for tile in range(tiles):
        span = slice(tile * DOCLEN, (tile + 1) * DOCLEN)
        swap(tile).wait_recv()
        total = (
            x_ref[span, :].astype(F32) + part[tile].astype(F32) + other[tile].astype(F32)
        )
        mean = jnp.mean(total, axis=1, keepdims=True)
        centred = total - mean
        spread = jnp.mean(centred * centred, axis=1, keepdims=True)
        hidden[...] = centred * lax.rsqrt(spread + 1e-07)
        out_ref[span, :] = (
            hidden[:, here] * gain_ref[:, here] + lnb_ref[:, here]
        ).astype(BF16)
        firsts = jnp.concatenate(
            [hidden[row : row + 1, :] for row in range(0, DOCLEN, SHORT)], axis=0
        )
        full = firsts * gain_ref[...] + lnb_ref[...]
        scores = jnp.sum(full * sw_ref[...], axis=1, keepdims=True)
        segments = DOCLEN // SHORT
        column = iota((segments, tiles * segments), 1) - tile * segments
        spread_scores = jnp.where(iota((segments, tiles * segments), 0) == column, scores, 0.0)
        seg_row = seg_row + jnp.sum(spread_scores, axis=0, keepdims=True)
    seg_ref[...] = seg_row

    def drain(step, carry):
        transfer(send_k, recv_k, 0, step).wait_send()
        transfer(send_v, recv_v, 1, step).wait_send()
        return carry

    lax.fori_loop(1, n, drain, 0)
    for tile in range(tiles):
        swap(tile).wait_send()


def shards(
    n,
    doc_x,
    doc_query,
    doc_key,
    doc_value,
    key_cache,
    value_cache,
    rel_embed,
    w_query,
    w_key,
    out_weight,
    ln_gain,
    ln_bias,
    score_weight,
    query_len,
    dev_query,
    page_table,
    tile_kind,
    rel_bucket,
):
    pages_here, page, cols = key_cache.shape
    queries, query_pages = page_table.shape
    tokens = query_pages * page
    block = pages_here // queries * page
    rows, model = doc_x.shape
    tiles = rows // DOCLEN
    heads_here = cols // HD

    vmem = pl.BlockSpec(memory_space=pltpu.VMEM)
    smem = pl.BlockSpec(memory_space=pltpu.SMEM)
    normed, seg = pl.pallas_call(
        functools.partial(kernel, n),
        out_shape=(
            jax.ShapeDtypeStruct((rows, model // 2), BF16),
            jax.ShapeDtypeStruct((1, rows // SHORT), F32),
        ),
        in_specs=[smem] * 3 + [vmem] * 7 + [pl.BlockSpec(memory_space=pl.ANY)] * 8,
        out_specs=(vmem, vmem),
        scratch_shapes=[
            pltpu.VMEM(rel_embed.shape, BF16),
            pltpu.VMEM(w_key.shape, BF16),
            pltpu.VMEM(w_query.shape, BF16),
            pltpu.VMEM((rows, cols), BF16),
            pltpu.VMEM((rows, cols), BF16),
            pltpu.VMEM((rows, cols), BF16),
            pltpu.VMEM(out_weight.shape, BF16),
            pltpu.VMEM((rows, model), BF16),
            pltpu.VMEM((queries, block, cols), BF16),
            pltpu.VMEM((queries, block, cols), BF16),
            pltpu.VMEM((n * block, cols), BF16),
            pltpu.VMEM((n * block, cols), BF16),
            pltpu.VMEM((tokens, cols), BF16),
            pltpu.VMEM((tokens, cols), BF16),
            pltpu.VMEM((2 * DOCLEN, cols), BF16),
            pltpu.VMEM((2 * DOCLEN, cols), BF16),
            pltpu.VMEM((tiles * heads_here, DOCLEN, DOCLEN), F32),
            pltpu.VMEM((tiles * heads_here, DOCLEN, tokens + DOCLEN), BF16),
            pltpu.VMEM((rows, cols), BF16),
            pltpu.VMEM((tiles, DOCLEN, model), BF16),
            pltpu.VMEM((tiles, DOCLEN, model), BF16),
            pltpu.VMEM((DOCLEN, model), F32),
            pltpu.SemaphoreType.DMA((8,)),
            pltpu.SemaphoreType.DMA((2, n)),
            pltpu.SemaphoreType.DMA((2, n)),
            pltpu.SemaphoreType.DMA((tiles,)),
            pltpu.SemaphoreType.DMA((tiles,)),
        ],
        compiler_params=pltpu.CompilerParams(
            collective_id=0, has_side_effects=True, vmem_limit_bytes=56 * 1024 * 1024
        ),
        cost_estimate=pl.CostEstimate(
            flops=8_000_000_000, bytes_accessed=12_000_000, transcendentals=5_000_000
        ),
    )(
        tile_kind,
        dev_query,
        query_len,
        page_table,
        key_cache,
        value_cache,
        rel_bucket[None, :],
        ln_gain[None, :],
        ln_bias[None, :],
        score_weight[None, :],
        rel_embed,
        w_key,
        w_query,
        doc_query,
        doc_key,
        doc_value,
        out_weight,
        doc_x,
    )
    return normed, seg.reshape(-1)


def solution(mesh):
    in_specs = (
        P("blk", None),
        P("blk", "head"),
        P("blk", "head"),
        P("blk", "head"),
        P("blk", None, "head"),
        P("blk", None, "head"),
        P(),
        P(None, "head"),
        P(None, "head"),
        P("head", None),
        P(),
        P(),
        P(),
        P(),
        P(),
        P(),
        P("blk"),
        P(),
    )
    out_specs = (P("blk", "head"), P("blk"))
    return jax.shard_map(
        functools.partial(shards, mesh.shape["blk"]),
        mesh=mesh,
        in_specs=in_specs,
        out_specs=out_specs,
        check_vma=False,
    )
```

```python
import functools

import jax
import jax.numpy as jnp
from jax import lax
from jax.experimental import pallas as pl
from jax.experimental.pallas import tpu as pltpu
from jax.sharding import PartitionSpec as P

HD = 64
DOCLEN = 256
SHORT = 16
PLANES = 4
MESH = pl.DeviceIdType.MESH
F32 = jnp.float32
BF16 = jnp.bfloat16
NEG = float("-inf")


def dot_t(a, b):
    return lax.dot_general(a, b, (((1,), (1,)), ((), ())), preferred_element_type=F32)


def skew(table):
    return pltpu.roll(table, 0, 1, stride=1, stride_axis=0)[:, DOCLEN:]


def kernel(
    n,
    kind_ref,
    asked_ref,
    length_ref,
    table_ref,
    keyc_ref,
    valuec_ref,
    bucket_ref,
    gain_ref,
    lnb_ref,
    sw_ref,
    embed_hbm,
    wk_hbm,
    wq_hbm,
    q_hbm,
    k_hbm,
    v_hbm,
    ow_hbm,
    x_hbm,
    out_ref,
    seg_ref,
    embed_ref,
    wk_ref,
    wq_ref,
    q_ref,
    k_ref,
    v_ref,
    ow_ref,
    x_ref,
    sorted_k,
    sorted_v,
    send_k,
    send_v,
    recv_k,
    recv_v,
    key_rel,
    query_rel,
    bias_ref,
    top_ref,
    acc,
    att,
    part,
    other,
    hidden,
    load_sem,
    line_send,
    line_recv,
    send_sem,
    recv_sem,
    pair_send,
    pair_recv,
    *passing,
):
    me = lax.axis_index("blk")
    width = n // PLANES
    plane, column = me // width, lax.rem(me, width)
    head = lax.axis_index("head")
    pages_here, page, cols = keyc_ref.shape
    queries, query_pages = table_ref.shape
    block = pages_here // queries * page
    rows = q_ref.shape[0]
    tiles = rows // DOCLEN
    pairs = cols // (2 * HD)
    model = x_ref.shape[1]
    local = pages_here * page
    tokens = PLANES * local
    factor = float(1.4426950408889634 / (3.0 * HD) ** 0.5)

    barrier = pltpu.get_barrier_semaphore()

    def in_plane(step):
        return plane * width + lax.rem(column + step, width)

    def greet(step, carry):
        pl.semaphore_signal(
            barrier, inc=1, device_id={"blk": in_plane(step)}, device_id_type=MESH
        )
        return carry

    lax.fori_loop(1, width, greet, 0)
    pl.semaphore_signal(barrier, inc=1, device_id={"head": 1 - head}, device_id_type=MESH)

    @pl.when(plane > 0)
    def _():
        pl.semaphore_signal(barrier, inc=1, device_id={"blk": me - width}, device_id_type=MESH)

    @pl.when(plane < PLANES - 1)
    def _():
        pl.semaphore_signal(barrier, inc=1, device_id={"blk": me + width}, device_id_type=MESH)

    loads = [
        pltpu.make_async_copy(source, target, load_sem.at[place])
        for place, (source, target) in enumerate(
            (
                (embed_hbm, embed_ref),
                (wk_hbm, wk_ref),
                (wq_hbm, wq_ref),
                (q_hbm, q_ref),
                (k_hbm, k_ref),
                (v_hbm, v_ref),
                (ow_hbm, ow_ref),
                (x_hbm, x_ref),
            )
        )
    ]
    for load in loads:
        load.start()

    def iota(shape, axis):
        return lax.broadcasted_iota(jnp.int32, shape, axis)

    square = (query_pages, query_pages)
    diagonal = iota(square, 0) == iota(square, 1)

    def upright(line):
        return jnp.sum(jnp.where(diagonal, line, 0), axis=1, keepdims=True)

    token = iota((1, local), 1)
    first = me * pages_here
    page_id = first + token // page
    target = jnp.zeros((1, local), jnp.int32)
    for query in range(queries):
        listed = upright(table_ref[query : query + 1, :])
        hit = jnp.sum((listed == page_id).astype(jnp.int32), axis=0, keepdims=True)
        before = jnp.sum(
            jnp.logical_and(listed >= first, listed < page_id).astype(jnp.int32),
            axis=0,
            keepdims=True,
        )
        target = target + hit * (query * block + before * page)
    target = target + token % page
    order = (iota((local, local), 0) == target).astype(BF16)
    for source, arranged in ((keyc_ref, sorted_k), (valuec_ref, sorted_v)):
        arranged[...] = (
            jnp.dot(order, source[...].reshape(local, cols), preferred_element_type=F32)
            .astype(BF16)
            .reshape(queries, block, cols)
        )

    below_me = (plane + PLANES - 1) // PLANES
    above_me = (2 * PLANES - 2 - plane) // PLANES
    pl.semaphore_wait(barrier, width + below_me + above_me)

    hops = PLANES - 1
    origin = ((sorted_k, sorted_v), (send_k, send_v), (recv_k, recv_v))

    def landing(which, way, hop):
        return passing[(which * 2 + way) * hops + hop - 1]

    def line(which, way, hop):
        return pltpu.make_async_remote_copy(
            src_ref=origin[0][which] if hop == 1 else landing(which, way, hop - 1),
            dst_ref=landing(which, way, hop),
            send_sem=line_send.at[which, way, hop - 1],
            recv_sem=line_recv.at[which, way, hop - 1],
            device_id={"blk": me + (width if way == 0 else -width)},
            device_id_type=MESH,
        )

    def source_plane(way, hop):
        return plane - hop if way == 0 else plane + hop

    def arrives(way, hop):
        return plane >= hop if way == 0 else plane + hop < PLANES

    def departs(way, hop):
        if way == 0:
            return jnp.logical_and(plane >= hop - 1, plane < PLANES - 1)
        return jnp.logical_and(plane + hop - 1 < PLANES, plane > 0)

    def deal(which, event, step):
        slot = event * width + step
        return pltpu.make_async_remote_copy(
            src_ref=origin[1][which].at[slot],
            dst_ref=origin[2][which].at[event, pl.ds(pl.multiple_of(column * block, block), block)],
            send_sem=send_sem.at[which, slot],
            recv_sem=recv_sem.at[which, slot],
            device_id={"blk": in_plane(step)},
            device_id_type=MESH,
        )

    def deal_all(which, event, held):
        def one(step, carry):
            origin[1][which][event * width + step] = held[asked_ref[in_plane(step)]]
            deal(which, event, step).start()
            return carry

        lax.fori_loop(1, width, one, 0)
        origin[2][which][event, pl.ds(pl.multiple_of(column * block, block), block), :] = held[
            asked_ref[me]
        ]

    def event_of(way, hop):
        return 1 + way * hops + hop - 1

    def send_line(which, way, hop):
        @pl.when(departs(way, hop))
        def _():
            line(which, way, hop).start()

    def handle(way, hop):
        @pl.when(arrives(way, hop))
        def _():
            for which in range(2):
                line(which, way, hop).wait_recv()
                if hop < hops:
                    send_line(which, way, hop + 1)
                deal_all(which, event_of(way, hop), landing(which, way, hop))

    for which in range(2):
        for way in range(2):
            send_line(which, way, 1)
    for which in range(2):
        deal_all(which, 0, origin[0][which])

    my_query = asked_ref[me]
    wanted = jnp.sum(
        jnp.where(iota((queries, query_pages), 0) == my_query, table_ref[...], 0),
        axis=0,
        keepdims=True,
    )
    rank = jnp.sum((wanted < upright(wanted)).astype(jnp.int32), axis=1, keepdims=True)
    spread_shape = (query_pages, tokens)
    place_id = jnp.sum(
        jnp.where(rank == iota(spread_shape, 1) // page, iota(spread_shape, 0), 0),
        axis=0,
        keepdims=True,
    )
    allowed_token = place_id * page + iota((1, tokens), 1) % page < length_ref[my_query]
    bias = jnp.where(allowed_token, 0.0, NEG).astype(F32)
    for index in range(PLANES):
        bias_ref[index] = bias[:, index * local : (index + 1) * local]

    buckets = embed_ref.shape[0]
    distances = bucket_ref.shape[1]
    flipped = iota((2 * DOCLEN, distances), 0) + iota((2 * DOCLEN, distances), 1) == distances
    bucket = jnp.sum(jnp.where(flipped, bucket_ref[...], 0), axis=1, keepdims=True)
    for load in loads[:3]:
        load.wait()
    picker = (bucket == iota((2 * DOCLEN, buckets), 1)).astype(BF16)
    for weight, table in ((wk_ref, key_rel), (wq_ref, query_rel)):
        projected = jnp.dot(embed_ref[...], weight[...], preferred_element_type=F32).astype(BF16)
        table[...] = jnp.dot(picker, projected, preferred_element_type=F32).astype(BF16)

    lane = lax.broadcasted_iota(jnp.int32, (1, 2 * HD), 1)
    halves = (lane < HD, lane >= HD)
    same_short = (
        lax.broadcasted_iota(jnp.int32, (DOCLEN, DOCLEN), 0) // SHORT
        == lax.broadcasted_iota(jnp.int32, (DOCLEN, DOCLEN), 1) // SHORT
    )

    def place(step):
        tile, pair = step // pairs, step % pairs
        tile_rows = pl.ds(pl.multiple_of(tile * DOCLEN, DOCLEN), DOCLEN)
        pair_cols = pl.ds(pl.multiple_of(pair * 2 * HD, 2 * HD), 2 * HD)
        return tile, tile_rows, pair_cols

    def own_scores(step, carry):
        tile, tile_rows, pair_cols = place(step)
        q = q_ref[tile_rows, pair_cols]
        k = k_ref[tile_rows, pair_cols]
        v = v_ref[tile_rows, pair_cols]
        kr = key_rel[:, pair_cols]
        qr = query_rel[:, pair_cols]
        allowed = jnp.where(same_short, 1, kind_ref[tile]) == 1
        for half in range(2):
            qh = jnp.where(halves[half], q, jnp.zeros_like(q))
            kh = jnp.where(halves[half], k, jnp.zeros_like(k))
            scores = dot_t(qh, k) + skew(dot_t(qh, kr)) + skew(dot_t(kh, qr)).T
            scores = jnp.where(allowed, scores, NEG)
            top = jnp.max(scores, axis=1, keepdims=True)
            weights = jnp.exp2((scores - top) * factor).astype(BF16)
            top_ref[step * 2 + half] = top
            acc[step * 2 + half] = jnp.dot(
                weights,
                jnp.where(halves[half], v, jnp.ones_like(v)),
                preferred_element_type=F32,
            )
        return carry

    for load in loads[3:]:
        load.wait()
    lax.fori_loop(0, tiles * pairs, own_scores, 0)

    def absorb(event, chunk):
        for which in range(2):
            lax.fori_loop(
                1, width, lambda step, carry: (deal(which, event, step).wait_recv(), carry)[1], 0
            )
        offset = bias_ref[chunk]

        def update(step, carry):
            tile, tile_rows, pair_cols = place(step)
            q = q_ref[tile_rows, pair_cols]
            keys = recv_k[event, :, pair_cols]
            values = recv_v[event, :, pair_cols]
            for half in range(2):
                qh = jnp.where(halves[half], q, jnp.zeros_like(q))
                scores = dot_t(qh, keys) + offset
                before = top_ref[step * 2 + half]
                top = jnp.maximum(before, jnp.max(scores, axis=1, keepdims=True))
                weights = jnp.exp2((scores - top) * factor).astype(BF16)
                top_ref[step * 2 + half] = top
                acc[step * 2 + half] = acc[step * 2 + half] * jnp.exp2(
                    (before - top) * factor
                ) + jnp.dot(
                    weights,
                    jnp.where(halves[half], values, jnp.ones_like(values)),
                    preferred_element_type=F32,
                )
            return carry

        lax.fori_loop(0, tiles * pairs, update, 0)

    def absorb_event(way, hop):
        @pl.when(arrives(way, hop))
        def _():
            absorb(event_of(way, hop), source_plane(way, hop))

    handle(0, 1)
    handle(1, 1)
    absorb(0, plane)
    for hop in range(1, hops + 1):
        for way in range(2):
            absorb_event(way, hop)
        if hop < hops:
            for way in range(2):
                handle(way, hop + 1)

    def finish(step, carry):
        tile, tile_rows, pair_cols = place(step)
        sums = [acc[step * 2], acc[step * 2 + 1]]
        above = jnp.where(halves[0], sums[0], sums[1])
        below = pltpu.roll(jnp.where(halves[0], sums[1], sums[0]), HD, 1)
        att[tile_rows, pair_cols] = (above / below).astype(BF16)
        return carry

    def swap(tile):
        return pltpu.make_async_remote_copy(
            src_ref=part.at[tile],
            dst_ref=other.at[tile],
            send_sem=pair_send.at[tile],
            recv_sem=pair_recv.at[tile],
            device_id={"head": 1 - head},
            device_id_type=MESH,
        )

    for tile in range(tiles):
        lax.fori_loop(tile * pairs, (tile + 1) * pairs, finish, 0)
        part[tile] = jnp.dot(
            att[tile * DOCLEN : (tile + 1) * DOCLEN, :], ow_ref[...], preferred_element_type=F32
        ).astype(BF16)
        swap(tile).start()

    seg_row = jnp.zeros(seg_ref.shape, F32)
    here = pl.ds(pl.multiple_of(head * (model // 2), model // 2), model // 2)
    for tile in range(tiles):
        span = slice(tile * DOCLEN, (tile + 1) * DOCLEN)
        swap(tile).wait_recv()
        total = (
            x_ref[span, :].astype(F32) + part[tile].astype(F32) + other[tile].astype(F32)
        )
        mean = jnp.mean(total, axis=1, keepdims=True)
        centred = total - mean
        spread = jnp.mean(centred * centred, axis=1, keepdims=True)
        hidden[...] = centred * lax.rsqrt(spread + 1e-07)
        out_ref[span, :] = (
            hidden[:, here] * gain_ref[:, here] + lnb_ref[:, here]
        ).astype(BF16)
        firsts = jnp.concatenate(
            [hidden[row : row + 1, :] for row in range(0, DOCLEN, SHORT)], axis=0
        )
        full = firsts * gain_ref[...] + lnb_ref[...]
        scores = jnp.sum(full * sw_ref[...], axis=1, keepdims=True)
        segments = DOCLEN // SHORT
        lane_id = iota((segments, tiles * segments), 1) - tile * segments
        spread_scores = jnp.where(iota((segments, tiles * segments), 0) == lane_id, scores, 0.0)
        seg_row = seg_row + jnp.sum(spread_scores, axis=0, keepdims=True)
    seg_ref[...] = seg_row

    def drain(event):
        for which in range(2):
            lax.fori_loop(
                1, width, lambda step, carry: (deal(which, event, step).wait_send(), carry)[1], 0
            )

    drain(0)
    for way in range(2):
        for hop in range(1, hops + 1):

            @pl.when(departs(way, hop))
            def _():
                for which in range(2):
                    line(which, way, hop).wait_send()

            @pl.when(arrives(way, hop))
            def _():
                drain(event_of(way, hop))

    for tile in range(tiles):
        swap(tile).wait_send()


def shards(
    n,
    doc_x,
    doc_query,
    doc_key,
    doc_value,
    key_cache,
    value_cache,
    rel_embed,
    w_query,
    w_key,
    out_weight,
    ln_gain,
    ln_bias,
    score_weight,
    query_len,
    dev_query,
    page_table,
    tile_kind,
    rel_bucket,
):
    pages_here, page, cols = key_cache.shape
    queries, query_pages = page_table.shape
    tokens = query_pages * page
    block = pages_here // queries * page
    rows, model = doc_x.shape
    width = n // PLANES
    events = 2 * PLANES - 1
    tiles = rows // DOCLEN
    heads_here = cols // HD

    vmem = pl.BlockSpec(memory_space=pltpu.VMEM)
    smem = pl.BlockSpec(memory_space=pltpu.SMEM)
    normed, seg = pl.pallas_call(
        functools.partial(kernel, n),
        out_shape=(
            jax.ShapeDtypeStruct((rows, model // 2), BF16),
            jax.ShapeDtypeStruct((1, rows // SHORT), F32),
        ),
        in_specs=[smem] * 3 + [vmem] * 7 + [pl.BlockSpec(memory_space=pl.ANY)] * 8,
        out_specs=(vmem, vmem),
        scratch_shapes=[
            pltpu.VMEM(rel_embed.shape, BF16),
            pltpu.VMEM(w_key.shape, BF16),
            pltpu.VMEM(w_query.shape, BF16),
            pltpu.VMEM((rows, cols), BF16),
            pltpu.VMEM((rows, cols), BF16),
            pltpu.VMEM((rows, cols), BF16),
            pltpu.VMEM(out_weight.shape, BF16),
            pltpu.VMEM((rows, model), BF16),
            pltpu.VMEM((queries, block, cols), BF16),
            pltpu.VMEM((queries, block, cols), BF16),
            pltpu.VMEM((events * width, block, cols), BF16),
            pltpu.VMEM((events * width, block, cols), BF16),
            pltpu.VMEM((events, width * block, cols), BF16),
            pltpu.VMEM((events, width * block, cols), BF16),
            pltpu.VMEM((2 * DOCLEN, cols), BF16),
            pltpu.VMEM((2 * DOCLEN, cols), BF16),
            pltpu.VMEM((PLANES, 1, tokens // PLANES), F32),
            pltpu.VMEM((tiles * heads_here, DOCLEN, 1), F32),
            pltpu.VMEM((tiles * heads_here, DOCLEN, 2 * HD), F32),
            pltpu.VMEM((rows, cols), BF16),
            pltpu.VMEM((tiles, DOCLEN, model), BF16),
            pltpu.VMEM((tiles, DOCLEN, model), BF16),
            pltpu.VMEM((DOCLEN, model), F32),
            pltpu.SemaphoreType.DMA((8,)),
            pltpu.SemaphoreType.DMA((2, 2, PLANES - 1)),
            pltpu.SemaphoreType.DMA((2, 2, PLANES - 1)),
            pltpu.SemaphoreType.DMA((2, events * width)),
            pltpu.SemaphoreType.DMA((2, events * width)),
            pltpu.SemaphoreType.DMA((tiles,)),
            pltpu.SemaphoreType.DMA((tiles,)),
        ]
        + [pltpu.VMEM((queries, block, cols), BF16)] * (4 * (PLANES - 1)),
        compiler_params=pltpu.CompilerParams(
            collective_id=0, has_side_effects=True, vmem_limit_bytes=56 * 1024 * 1024
        ),
        cost_estimate=pl.CostEstimate(
            flops=8_000_000_000, bytes_accessed=12_000_000, transcendentals=5_000_000
        ),
    )(
        tile_kind,
        dev_query,
        query_len,
        page_table,
        key_cache,
        value_cache,
        rel_bucket[None, :],
        ln_gain[None, :],
        ln_bias[None, :],
        score_weight[None, :],
        rel_embed,
        w_key,
        w_query,
        doc_query,
        doc_key,
        doc_value,
        out_weight,
        doc_x,
    )
    return normed, seg.reshape(-1)


def solution(mesh):
    in_specs = (
        P("blk", None),
        P("blk", "head"),
        P("blk", "head"),
        P("blk", "head"),
        P("blk", None, "head"),
        P("blk", None, "head"),
        P(),
        P(None, "head"),
        P(None, "head"),
        P("head", None),
        P(),
        P(),
        P(),
        P(),
        P(),
        P(),
        P("blk"),
        P(),
    )
    out_specs = (P("blk", "head"), P("blk"))
    return jax.shard_map(
        functools.partial(shards, mesh.shape["blk"]),
        mesh=mesh,
        in_specs=in_specs,
        out_specs=out_specs,
        check_vma=False,
    )
```

```python
import functools

import jax
import jax.numpy as jnp
from jax import lax
from jax.experimental import pallas as pl
from jax.experimental.pallas import tpu as pltpu
from jax.sharding import PartitionSpec as P

HD = 64
DOCLEN = 256
SHORT = 16
PLANES = 4
MESH = pl.DeviceIdType.MESH
F32 = jnp.float32
BF16 = jnp.bfloat16
NEG = float("-inf")


def dot_t(a, b):
    return lax.dot_general(a, b, (((1,), (1,)), ((), ())), preferred_element_type=F32)


def skew(table):
    return pltpu.roll(table, 0, 1, stride=1, stride_axis=0)[:, DOCLEN:]


def kernel(
    n,
    kind_ref,
    asked_ref,
    length_ref,
    table_ref,
    keyc_ref,
    valuec_ref,
    bucket_ref,
    gain_ref,
    lnb_ref,
    sw_ref,
    embed_hbm,
    wk_hbm,
    wq_hbm,
    q_hbm,
    k_hbm,
    v_hbm,
    ow_hbm,
    x_hbm,
    out_ref,
    seg_ref,
    embed_ref,
    wk_ref,
    wq_ref,
    q_ref,
    k_ref,
    v_ref,
    ow_ref,
    x_ref,
    sorted_k,
    sorted_v,
    send_k,
    send_v,
    recv_k,
    recv_v,
    key_rel,
    query_rel,
    bias_ref,
    top_ref,
    acc,
    att,
    part,
    other,
    hidden,
    load_sem,
    line_send,
    line_recv,
    send_sem,
    recv_sem,
    pair_send,
    pair_recv,
    *passing,
):
    me = lax.axis_index("blk")
    width = n // PLANES
    plane, column = me // width, lax.rem(me, width)
    head = lax.axis_index("head")
    pages_here, page, cols = keyc_ref.shape
    queries, query_pages = table_ref.shape
    block = pages_here // queries * page
    rows = q_ref.shape[0]
    tiles = rows // DOCLEN
    pairs = cols // (2 * HD)
    model = x_ref.shape[1]
    local = pages_here * page
    tokens = PLANES * local
    factor = float(1.4426950408889634 / (3.0 * HD) ** 0.5)

    barrier = pltpu.get_barrier_semaphore()

    def in_plane(step):
        return plane * width + lax.rem(column + step, width)

    def greet(step, carry):
        pl.semaphore_signal(
            barrier, inc=1, device_id={"blk": in_plane(step)}, device_id_type=MESH
        )
        return carry

    lax.fori_loop(1, width, greet, 0)
    pl.semaphore_signal(barrier, inc=1, device_id={"head": 1 - head}, device_id_type=MESH)

    @pl.when(plane > 0)
    def _():
        pl.semaphore_signal(barrier, inc=1, device_id={"blk": me - width}, device_id_type=MESH)

    @pl.when(plane < PLANES - 1)
    def _():
        pl.semaphore_signal(barrier, inc=1, device_id={"blk": me + width}, device_id_type=MESH)

    loads = [
        pltpu.make_async_copy(source, target, load_sem.at[place])
        for place, (source, target) in enumerate(
            (
                (embed_hbm, embed_ref),
                (wk_hbm, wk_ref),
                (wq_hbm, wq_ref),
                (q_hbm, q_ref),
                (k_hbm, k_ref),
                (v_hbm, v_ref),
                (ow_hbm, ow_ref),
                (x_hbm, x_ref),
            )
        )
    ]
    for load in loads:
        load.start()

    def iota(shape, axis):
        return lax.broadcasted_iota(jnp.int32, shape, axis)

    square = (query_pages, query_pages)
    diagonal = iota(square, 0) == iota(square, 1)

    def upright(line):
        return jnp.sum(jnp.where(diagonal, line, 0), axis=1, keepdims=True)

    token = iota((1, local), 1)
    first = me * pages_here
    page_id = first + token // page
    target = jnp.zeros((1, local), jnp.int32)
    for query in range(queries):
        listed = upright(table_ref[query : query + 1, :])
        hit = jnp.sum((listed == page_id).astype(jnp.int32), axis=0, keepdims=True)
        before = jnp.sum(
            jnp.logical_and(listed >= first, listed < page_id).astype(jnp.int32),
            axis=0,
            keepdims=True,
        )
        target = target + hit * (query * block + before * page)
    target = target + token % page
    order = (iota((local, local), 0) == target).astype(BF16)
    for source, arranged in ((keyc_ref, sorted_k), (valuec_ref, sorted_v)):
        arranged[...] = (
            jnp.dot(order, source[...].reshape(local, cols), preferred_element_type=F32)
            .astype(BF16)
            .reshape(queries, block, cols)
        )

    below_me = (plane + PLANES - 1) // PLANES
    above_me = (2 * PLANES - 2 - plane) // PLANES
    pl.semaphore_wait(barrier, width + below_me + above_me)

    hops = PLANES - 1
    origin = ((sorted_k, sorted_v), (send_k, send_v), (recv_k, recv_v))

    def landing(which, way, hop):
        return passing[(which * 2 + way) * hops + hop - 1]

    def line(which, way, hop):
        return pltpu.make_async_remote_copy(
            src_ref=origin[0][which] if hop == 1 else landing(which, way, hop - 1),
            dst_ref=landing(which, way, hop),
            send_sem=line_send.at[which, way, hop - 1],
            recv_sem=line_recv.at[which, way, hop - 1],
            device_id={"blk": me + (width if way == 0 else -width)},
            device_id_type=MESH,
        )

    def source_plane(way, hop):
        return plane - hop if way == 0 else plane + hop

    def arrives(way, hop):
        return plane >= hop if way == 0 else plane + hop < PLANES

    def departs(way, hop):
        if way == 0:
            return jnp.logical_and(plane >= hop - 1, plane < PLANES - 1)
        return jnp.logical_and(plane + hop - 1 < PLANES, plane > 0)

    def deal(which, event, step):
        slot = event * width + step
        return pltpu.make_async_remote_copy(
            src_ref=origin[1][which].at[slot],
            dst_ref=origin[2][which].at[event, pl.ds(pl.multiple_of(column * block, block), block)],
            send_sem=send_sem.at[which, slot],
            recv_sem=recv_sem.at[which, slot],
            device_id={"blk": in_plane(step)},
            device_id_type=MESH,
        )

    def deal_all(which, event, held):
        def one(step, carry):
            origin[1][which][event * width + step] = held[asked_ref[in_plane(step)]]
            deal(which, event, step).start()
            return carry

        lax.fori_loop(1, width, one, 0)
        origin[2][which][event, pl.ds(pl.multiple_of(column * block, block), block), :] = held[
            asked_ref[me]
        ]

    def event_of(way, hop):
        return 1 + way * hops + hop - 1

    def send_line(which, way, hop):
        @pl.when(departs(way, hop))
        def _():
            line(which, way, hop).start()

    def handle(way, hop):
        @pl.when(arrives(way, hop))
        def _():
            for which in range(2):
                line(which, way, hop).wait_recv()
                if hop < hops:
                    send_line(which, way, hop + 1)
                deal_all(which, event_of(way, hop), landing(which, way, hop))

    for which in range(2):
        for way in range(2):
            send_line(which, way, 1)
    for which in range(2):
        deal_all(which, 0, origin[0][which])

    my_query = asked_ref[me]
    wanted = jnp.sum(
        jnp.where(iota((queries, query_pages), 0) == my_query, table_ref[...], 0),
        axis=0,
        keepdims=True,
    )
    rank = jnp.sum((wanted < upright(wanted)).astype(jnp.int32), axis=1, keepdims=True)
    spread_shape = (query_pages, tokens)
    place_id = jnp.sum(
        jnp.where(rank == iota(spread_shape, 1) // page, iota(spread_shape, 0), 0),
        axis=0,
        keepdims=True,
    )
    allowed_token = place_id * page + iota((1, tokens), 1) % page < length_ref[my_query]
    bias = jnp.where(allowed_token, 0.0, NEG).astype(F32)
    for index in range(PLANES):
        bias_ref[index] = bias[:, index * local : (index + 1) * local]

    buckets = embed_ref.shape[0]
    distances = bucket_ref.shape[1]
    flipped = iota((2 * DOCLEN, distances), 0) + iota((2 * DOCLEN, distances), 1) == distances
    bucket = jnp.sum(jnp.where(flipped, bucket_ref[...], 0), axis=1, keepdims=True)
    for load in loads[:3]:
        load.wait()
    picker = (bucket == iota((2 * DOCLEN, buckets), 1)).astype(BF16)
    for weight, table in ((wk_ref, key_rel), (wq_ref, query_rel)):
        projected = jnp.dot(embed_ref[...], weight[...], preferred_element_type=F32).astype(BF16)
        table[...] = jnp.dot(picker, projected, preferred_element_type=F32).astype(BF16)

    lane = lax.broadcasted_iota(jnp.int32, (1, 2 * HD), 1)
    halves = (lane < HD, lane >= HD)
    same_short = (
        lax.broadcasted_iota(jnp.int32, (DOCLEN, DOCLEN), 0) // SHORT
        == lax.broadcasted_iota(jnp.int32, (DOCLEN, DOCLEN), 1) // SHORT
    )

    def pair_span(pair):
        return pl.ds(pl.multiple_of(pair * 2 * HD, 2 * HD), 2 * HD)

    def tile_span(tile):
        return slice(tile * DOCLEN, (tile + 1) * DOCLEN)

    def own_scores(pair, carry):
        pair_cols = pair_span(pair)
        kr = key_rel[:, pair_cols]
        qr = query_rel[:, pair_cols]
        results = []
        for tile in range(tiles):
            q = q_ref[tile_span(tile), pair_cols]
            k = k_ref[tile_span(tile), pair_cols]
            v = v_ref[tile_span(tile), pair_cols]
            allowed = jnp.where(same_short, 1, kind_ref[tile]) == 1
            for half in range(2):
                qh = jnp.where(halves[half], q, jnp.zeros_like(q))
                kh = jnp.where(halves[half], k, jnp.zeros_like(k))
                scores = dot_t(qh, k) + skew(dot_t(qh, kr)) + skew(dot_t(kh, qr)).T
                scores = jnp.where(allowed, scores, NEG)
                top = jnp.max(scores, axis=1, keepdims=True)
                weights = jnp.exp2((scores - top) * factor).astype(BF16)
                total = jnp.dot(
                    weights,
                    jnp.where(halves[half], v, jnp.ones_like(v)),
                    preferred_element_type=F32,
                )
                results.append((tile, half, top, total))
        for tile, half, top, total in results:
            top_ref[pair * 2 + half, tile_span(tile), :] = top
            acc[pair * 2 + half, tile_span(tile), :] = total
        return carry

    for load in loads[3:]:
        load.wait()
    lax.fori_loop(0, pairs // 2, own_scores, 0)
    handle(0, 1)
    handle(1, 1)
    lax.fori_loop(pairs // 2, pairs, own_scores, 0)

    def absorb(event, chunk):
        for which in range(2):
            lax.fori_loop(
                1, width, lambda step, carry: (deal(which, event, step).wait_recv(), carry)[1], 0
            )
        offset = bias_ref[chunk]

        def update(step, carry):
            results = []
            for pair in (step * 2, step * 2 + 1):
                pair_cols = pair_span(pair)
                q = q_ref[:, pair_cols]
                keys = recv_k[event, :, pair_cols]
                values = recv_v[event, :, pair_cols]
                for half in range(2):
                    qh = jnp.where(halves[half], q, jnp.zeros_like(q))
                    scores = dot_t(qh, keys) + offset
                    before = top_ref[pair * 2 + half]
                    top = jnp.maximum(before, jnp.max(scores, axis=1, keepdims=True))
                    weights = jnp.exp2((scores - top) * factor).astype(BF16)
                    total = acc[pair * 2 + half] * jnp.exp2((before - top) * factor) + jnp.dot(
                        weights,
                        jnp.where(halves[half], values, jnp.ones_like(values)),
                        preferred_element_type=F32,
                    )
                    results.append((pair * 2 + half, top, total))
            for index, top, total in results:
                top_ref[index] = top
                acc[index] = total
            return carry

        lax.fori_loop(0, pairs // 2, update, 0)

    def absorb_event(way, hop):
        @pl.when(arrives(way, hop))
        def _():
            absorb(event_of(way, hop), source_plane(way, hop))

    absorb(0, plane)
    for hop in range(1, hops + 1):
        if hop < hops:
            for way in range(2):
                handle(way, hop + 1)
        for way in range(2):
            absorb_event(way, hop)

    def finish(tile):
        for pair in range(pairs):
            sums = [acc[pair * 2 + half, tile_span(tile), :] for half in range(2)]
            above = jnp.where(halves[0], sums[0], sums[1])
            below = pltpu.roll(jnp.where(halves[0], sums[1], sums[0]), HD, 1)
            att[tile_span(tile), pair * 2 * HD : (pair + 1) * 2 * HD] = (above / below).astype(
                BF16
            )

    def swap(tile):
        return pltpu.make_async_remote_copy(
            src_ref=part.at[tile],
            dst_ref=other.at[tile],
            send_sem=pair_send.at[tile],
            recv_sem=pair_recv.at[tile],
            device_id={"head": 1 - head},
            device_id_type=MESH,
        )

    for tile in range(tiles):
        finish(tile)
        part[tile] = jnp.dot(
            att[tile * DOCLEN : (tile + 1) * DOCLEN, :], ow_ref[...], preferred_element_type=F32
        ).astype(BF16)
        swap(tile).start()

    seg_row = jnp.zeros(seg_ref.shape, F32)
    here = pl.ds(pl.multiple_of(head * (model // 2), model // 2), model // 2)
    for tile in range(tiles):
        span = slice(tile * DOCLEN, (tile + 1) * DOCLEN)
        swap(tile).wait_recv()
        total = (
            x_ref[span, :].astype(F32) + part[tile].astype(F32) + other[tile].astype(F32)
        )
        mean = jnp.mean(total, axis=1, keepdims=True)
        centred = total - mean
        spread = jnp.mean(centred * centred, axis=1, keepdims=True)
        hidden[...] = centred * lax.rsqrt(spread + 1e-07)
        out_ref[span, :] = (
            hidden[:, here] * gain_ref[:, here] + lnb_ref[:, here]
        ).astype(BF16)
        firsts = jnp.concatenate(
            [hidden[row : row + 1, :] for row in range(0, DOCLEN, SHORT)], axis=0
        )
        full = firsts * gain_ref[...] + lnb_ref[...]
        scores = jnp.sum(full * sw_ref[...], axis=1, keepdims=True)
        segments = DOCLEN // SHORT
        lane_id = iota((segments, tiles * segments), 1) - tile * segments
        spread_scores = jnp.where(iota((segments, tiles * segments), 0) == lane_id, scores, 0.0)
        seg_row = seg_row + jnp.sum(spread_scores, axis=0, keepdims=True)
    seg_ref[...] = seg_row

    def drain(event):
        for which in range(2):
            lax.fori_loop(
                1, width, lambda step, carry: (deal(which, event, step).wait_send(), carry)[1], 0
            )

    drain(0)
    for way in range(2):
        for hop in range(1, hops + 1):

            @pl.when(departs(way, hop))
            def _():
                for which in range(2):
                    line(which, way, hop).wait_send()

            @pl.when(arrives(way, hop))
            def _():
                drain(event_of(way, hop))

    for tile in range(tiles):
        swap(tile).wait_send()


def shards(
    n,
    doc_x,
    doc_query,
    doc_key,
    doc_value,
    key_cache,
    value_cache,
    rel_embed,
    w_query,
    w_key,
    out_weight,
    ln_gain,
    ln_bias,
    score_weight,
    query_len,
    dev_query,
    page_table,
    tile_kind,
    rel_bucket,
):
    pages_here, page, cols = key_cache.shape
    queries, query_pages = page_table.shape
    tokens = query_pages * page
    block = pages_here // queries * page
    rows, model = doc_x.shape
    width = n // PLANES
    events = 2 * PLANES - 1
    tiles = rows // DOCLEN
    heads_here = cols // HD

    vmem = pl.BlockSpec(memory_space=pltpu.VMEM)
    smem = pl.BlockSpec(memory_space=pltpu.SMEM)
    normed, seg = pl.pallas_call(
        functools.partial(kernel, n),
        out_shape=(
            jax.ShapeDtypeStruct((rows, model // 2), BF16),
            jax.ShapeDtypeStruct((1, rows // SHORT), F32),
        ),
        in_specs=[smem] * 3 + [vmem] * 7 + [pl.BlockSpec(memory_space=pl.ANY)] * 8,
        out_specs=(vmem, vmem),
        scratch_shapes=[
            pltpu.VMEM(rel_embed.shape, BF16),
            pltpu.VMEM(w_key.shape, BF16),
            pltpu.VMEM(w_query.shape, BF16),
            pltpu.VMEM((rows, cols), BF16),
            pltpu.VMEM((rows, cols), BF16),
            pltpu.VMEM((rows, cols), BF16),
            pltpu.VMEM(out_weight.shape, BF16),
            pltpu.VMEM((rows, model), BF16),
            pltpu.VMEM((queries, block, cols), BF16),
            pltpu.VMEM((queries, block, cols), BF16),
            pltpu.VMEM((events * width, block, cols), BF16),
            pltpu.VMEM((events * width, block, cols), BF16),
            pltpu.VMEM((events, width * block, cols), BF16),
            pltpu.VMEM((events, width * block, cols), BF16),
            pltpu.VMEM((2 * DOCLEN, cols), BF16),
            pltpu.VMEM((2 * DOCLEN, cols), BF16),
            pltpu.VMEM((PLANES, 1, tokens // PLANES), F32),
            pltpu.VMEM((heads_here, rows, 1), F32),
            pltpu.VMEM((heads_here, rows, 2 * HD), F32),
            pltpu.VMEM((rows, cols), BF16),
            pltpu.VMEM((tiles, DOCLEN, model), BF16),
            pltpu.VMEM((tiles, DOCLEN, model), BF16),
            pltpu.VMEM((DOCLEN, model), F32),
            pltpu.SemaphoreType.DMA((8,)),
            pltpu.SemaphoreType.DMA((2, 2, PLANES - 1)),
            pltpu.SemaphoreType.DMA((2, 2, PLANES - 1)),
            pltpu.SemaphoreType.DMA((2, events * width)),
            pltpu.SemaphoreType.DMA((2, events * width)),
            pltpu.SemaphoreType.DMA((tiles,)),
            pltpu.SemaphoreType.DMA((tiles,)),
        ]
        + [pltpu.VMEM((queries, block, cols), BF16)] * (4 * (PLANES - 1)),
        compiler_params=pltpu.CompilerParams(
            collective_id=0, has_side_effects=True, vmem_limit_bytes=56 * 1024 * 1024
        ),
        cost_estimate=pl.CostEstimate(
            flops=8_000_000_000, bytes_accessed=12_000_000, transcendentals=5_000_000
        ),
    )(
        tile_kind,
        dev_query,
        query_len,
        page_table,
        key_cache,
        value_cache,
        rel_bucket[None, :],
        ln_gain[None, :],
        ln_bias[None, :],
        score_weight[None, :],
        rel_embed,
        w_key,
        w_query,
        doc_query,
        doc_key,
        doc_value,
        out_weight,
        doc_x,
    )
    return normed, seg.reshape(-1)


def solution(mesh):
    in_specs = (
        P("blk", None),
        P("blk", "head"),
        P("blk", "head"),
        P("blk", "head"),
        P("blk", None, "head"),
        P("blk", None, "head"),
        P(),
        P(None, "head"),
        P(None, "head"),
        P("head", None),
        P(),
        P(),
        P(),
        P(),
        P(),
        P(),
        P("blk"),
        P(),
    )
    out_specs = (P("blk", "head"), P("blk"))
    return jax.shard_map(
        functools.partial(shards, mesh.shape["blk"]),
        mesh=mesh,
        in_specs=in_specs,
        out_specs=out_specs,
        check_vma=False,
    )
```

```python
import functools

import jax
import jax.numpy as jnp
from jax import lax
from jax.experimental import pallas as pl
from jax.experimental.pallas import tpu as pltpu
from jax.sharding import PartitionSpec as P

HD = 64
DOCLEN = 256
SHORT = 16
PLANES = 4
MESH = pl.DeviceIdType.MESH
F32 = jnp.float32
BF16 = jnp.bfloat16
NEG = float("-inf")


def dot_t(a, b):
    return lax.dot_general(a, b, (((1,), (1,)), ((), ())), preferred_element_type=F32)


def skew(table):
    return pltpu.roll(table, 0, 1, stride=1, stride_axis=0)[:, DOCLEN:]


def kernel(
    n,
    kind_ref,
    asked_ref,
    length_ref,
    table_ref,
    keyc_ref,
    valuec_ref,
    bucket_ref,
    gain_ref,
    lnb_ref,
    sw_ref,
    embed_hbm,
    wk_hbm,
    wq_hbm,
    q_hbm,
    k_hbm,
    v_hbm,
    ow_hbm,
    x_hbm,
    out_ref,
    seg_ref,
    embed_ref,
    wk_ref,
    wq_ref,
    q_ref,
    k_ref,
    v_ref,
    ow_ref,
    x_ref,
    sorted_k,
    sorted_v,
    send_k,
    send_v,
    recv_k,
    recv_v,
    key_rel,
    query_rel,
    bias_ref,
    top_ref,
    acc,
    probs,
    att,
    part,
    other,
    hidden,
    load_sem,
    line_send,
    line_recv,
    send_sem,
    recv_sem,
    pair_send,
    pair_recv,
    *passing,
):
    me = lax.axis_index("blk")
    width = n // PLANES
    plane, column = me // width, lax.rem(me, width)
    head = lax.axis_index("head")
    pages_here, page, cols = keyc_ref.shape
    queries, query_pages = table_ref.shape
    block = pages_here // queries * page
    rows = q_ref.shape[0]
    tiles = rows // DOCLEN
    pairs = cols // (2 * HD)
    model = x_ref.shape[1]
    local = pages_here * page
    tokens = PLANES * local
    factor = float(1.4426950408889634 / (3.0 * HD) ** 0.5)

    barrier = pltpu.get_barrier_semaphore()

    def in_plane(step):
        return plane * width + lax.rem(column + step, width)

    def greet(step, carry):
        pl.semaphore_signal(
            barrier, inc=1, device_id={"blk": in_plane(step)}, device_id_type=MESH
        )
        return carry

    lax.fori_loop(1, width, greet, 0)
    pl.semaphore_signal(barrier, inc=1, device_id={"head": 1 - head}, device_id_type=MESH)

    @pl.when(plane > 0)
    def _():
        pl.semaphore_signal(barrier, inc=1, device_id={"blk": me - width}, device_id_type=MESH)

    @pl.when(plane < PLANES - 1)
    def _():
        pl.semaphore_signal(barrier, inc=1, device_id={"blk": me + width}, device_id_type=MESH)

    loads = [
        pltpu.make_async_copy(source, target, load_sem.at[place])
        for place, (source, target) in enumerate(
            (
                (embed_hbm, embed_ref),
                (wk_hbm, wk_ref),
                (wq_hbm, wq_ref),
                (q_hbm, q_ref),
                (k_hbm, k_ref),
                (v_hbm, v_ref),
                (ow_hbm, ow_ref),
                (x_hbm, x_ref),
            )
        )
    ]
    for load in loads:
        load.start()

    def iota(shape, axis):
        return lax.broadcasted_iota(jnp.int32, shape, axis)

    square = (query_pages, query_pages)
    diagonal = iota(square, 0) == iota(square, 1)

    def upright(line):
        return jnp.sum(jnp.where(diagonal, line, 0), axis=1, keepdims=True)

    token = iota((1, local), 1)
    first = me * pages_here
    page_id = first + token // page
    target = jnp.zeros((1, local), jnp.int32)
    for query in range(queries):
        listed = upright(table_ref[query : query + 1, :])
        hit = jnp.sum((listed == page_id).astype(jnp.int32), axis=0, keepdims=True)
        before = jnp.sum(
            jnp.logical_and(listed >= first, listed < page_id).astype(jnp.int32),
            axis=0,
            keepdims=True,
        )
        target = target + hit * (query * block + before * page)
    target = target + token % page
    order = (iota((local, local), 0) == target).astype(BF16)
    for source, arranged in ((keyc_ref, sorted_k), (valuec_ref, sorted_v)):
        arranged[...] = (
            jnp.dot(order, source[...].reshape(local, cols), preferred_element_type=F32)
            .astype(BF16)
            .reshape(queries, block, cols)
        )

    below_me = (plane + PLANES - 1) // PLANES
    above_me = (2 * PLANES - 2 - plane) // PLANES
    pl.semaphore_wait(barrier, width + below_me + above_me)

    hops = PLANES - 1
    origin = ((sorted_k, sorted_v), (send_k, send_v), (recv_k, recv_v))

    def landing(which, way, hop):
        return passing[(which * 2 + way) * hops + hop - 1]

    def line(which, way, hop):
        return pltpu.make_async_remote_copy(
            src_ref=origin[0][which] if hop == 1 else landing(which, way, hop - 1),
            dst_ref=landing(which, way, hop),
            send_sem=line_send.at[which, way, hop - 1],
            recv_sem=line_recv.at[which, way, hop - 1],
            device_id={"blk": me + (width if way == 0 else -width)},
            device_id_type=MESH,
        )

    def source_plane(way, hop):
        return plane - hop if way == 0 else plane + hop

    def arrives(way, hop):
        return plane >= hop if way == 0 else plane + hop < PLANES

    def departs(way, hop):
        if way == 0:
            return jnp.logical_and(plane >= hop - 1, plane < PLANES - 1)
        return jnp.logical_and(plane + hop - 1 < PLANES, plane > 0)

    def deal(which, event, step):
        slot = event * width + step
        return pltpu.make_async_remote_copy(
            src_ref=origin[1][which].at[slot],
            dst_ref=origin[2][which].at[event, pl.ds(pl.multiple_of(column * block, block), block)],
            send_sem=send_sem.at[which, slot],
            recv_sem=recv_sem.at[which, slot],
            device_id={"blk": in_plane(step)},
            device_id_type=MESH,
        )

    def deal_all(which, event, held):
        def one(step, carry):
            origin[1][which][event * width + step] = held[asked_ref[in_plane(step)]]
            deal(which, event, step).start()
            return carry

        lax.fori_loop(1, width, one, 0)
        origin[2][which][event, pl.ds(pl.multiple_of(column * block, block), block), :] = held[
            asked_ref[me]
        ]

    def event_of(way, hop):
        return 1 + way * hops + hop - 1

    def send_line(which, way, hop):
        @pl.when(departs(way, hop))
        def _():
            line(which, way, hop).start()

    def handle(way, hop, kinds=(0, 1)):
        @pl.when(arrives(way, hop))
        def _():
            for which in kinds:
                line(which, way, hop).wait_recv()
                if hop < hops:
                    send_line(which, way, hop + 1)
                deal_all(which, event_of(way, hop), landing(which, way, hop))

    for which in range(2):
        for way in range(2):
            send_line(which, way, 1)
    for which in range(2):
        deal_all(which, 0, origin[0][which])

    my_query = asked_ref[me]
    wanted = jnp.sum(
        jnp.where(iota((queries, query_pages), 0) == my_query, table_ref[...], 0),
        axis=0,
        keepdims=True,
    )
    rank = jnp.sum((wanted < upright(wanted)).astype(jnp.int32), axis=1, keepdims=True)
    spread_shape = (query_pages, tokens)
    place_id = jnp.sum(
        jnp.where(rank == iota(spread_shape, 1) // page, iota(spread_shape, 0), 0),
        axis=0,
        keepdims=True,
    )
    allowed_token = place_id * page + iota((1, tokens), 1) % page < length_ref[my_query]
    bias = jnp.where(allowed_token, 0.0, NEG).astype(F32)
    for index in range(PLANES):
        bias_ref[index] = bias[:, index * local : (index + 1) * local]

    buckets = embed_ref.shape[0]
    distances = bucket_ref.shape[1]
    flipped = iota((2 * DOCLEN, distances), 0) + iota((2 * DOCLEN, distances), 1) == distances
    bucket = jnp.sum(jnp.where(flipped, bucket_ref[...], 0), axis=1, keepdims=True)
    for load in loads[:3]:
        load.wait()
    picker = (bucket == iota((2 * DOCLEN, buckets), 1)).astype(BF16)
    for weight, table in ((wk_ref, key_rel), (wq_ref, query_rel)):
        projected = jnp.dot(embed_ref[...], weight[...], preferred_element_type=F32).astype(BF16)
        table[...] = jnp.dot(picker, projected, preferred_element_type=F32).astype(BF16)

    lane = lax.broadcasted_iota(jnp.int32, (1, 2 * HD), 1)
    halves = (lane < HD, lane >= HD)
    same_short = (
        lax.broadcasted_iota(jnp.int32, (DOCLEN, DOCLEN), 0) // SHORT
        == lax.broadcasted_iota(jnp.int32, (DOCLEN, DOCLEN), 1) // SHORT
    )

    def pair_span(pair):
        return pl.ds(pl.multiple_of(pair * 2 * HD, 2 * HD), 2 * HD)

    def tile_span(tile):
        return slice(tile * DOCLEN, (tile + 1) * DOCLEN)

    def own_scores(pair, carry):
        pair_cols = pair_span(pair)
        kr = key_rel[:, pair_cols]
        qr = query_rel[:, pair_cols]
        results = []
        for tile in range(tiles):
            q = q_ref[tile_span(tile), pair_cols]
            k = k_ref[tile_span(tile), pair_cols]
            v = v_ref[tile_span(tile), pair_cols]
            allowed = jnp.where(same_short, 1, kind_ref[tile]) == 1
            for half in range(2):
                qh = jnp.where(halves[half], q, jnp.zeros_like(q))
                kh = jnp.where(halves[half], k, jnp.zeros_like(k))
                scores = dot_t(qh, k) + skew(dot_t(qh, kr)) + skew(dot_t(kh, qr)).T
                scores = jnp.where(allowed, scores, NEG)
                top = jnp.max(scores, axis=1, keepdims=True)
                weights = jnp.exp2((scores - top) * factor).astype(BF16)
                total = jnp.dot(
                    weights,
                    jnp.where(halves[half], v, jnp.ones_like(v)),
                    preferred_element_type=F32,
                )
                results.append((tile, half, top, total))
        for tile, half, top, total in results:
            top_ref[pair * 2 + half, tile_span(tile), :] = top
            acc[pair * 2 + half, tile_span(tile), :] = total
        return carry

    for load in loads[3:]:
        load.wait()
    lax.fori_loop(0, pairs // 2, own_scores, 0)
    handle(0, 1)
    handle(1, 1)
    lax.fori_loop(pairs // 2, pairs, own_scores, 0)

    def absorb(event, chunk):
        for which in range(2):
            lax.fori_loop(
                1, width, lambda step, carry: (deal(which, event, step).wait_recv(), carry)[1], 0
            )
        offset = bias_ref[chunk]

        def update(step, carry):
            results = []
            for pair in (step * 2, step * 2 + 1):
                pair_cols = pair_span(pair)
                q = q_ref[:, pair_cols]
                keys = recv_k[event, :, pair_cols]
                values = recv_v[event, :, pair_cols]
                for half in range(2):
                    qh = jnp.where(halves[half], q, jnp.zeros_like(q))
                    scores = dot_t(qh, keys) + offset
                    before = top_ref[pair * 2 + half]
                    top = jnp.maximum(before, jnp.max(scores, axis=1, keepdims=True))
                    weights = jnp.exp2((scores - top) * factor).astype(BF16)
                    total = acc[pair * 2 + half] * jnp.exp2((before - top) * factor) + jnp.dot(
                        weights,
                        jnp.where(halves[half], values, jnp.ones_like(values)),
                        preferred_element_type=F32,
                    )
                    results.append((pair * 2 + half, top, total))
            for index, top, total in results:
                top_ref[index] = top
                acc[index] = total
            return carry

        lax.fori_loop(0, pairs // 2, update, 0)

    def landed(which, event):
        lax.fori_loop(
            1, width, lambda step, carry: (deal(which, event, step).wait_recv(), carry)[1], 0
        )

    def weigh_last(event, chunk):
        landed(0, event)
        offset = bias_ref[chunk]

        def update(step, carry):
            results = []
            for pair in (step * 2, step * 2 + 1):
                pair_cols = pair_span(pair)
                q = q_ref[:, pair_cols]
                keys = recv_k[event, :, pair_cols]
                for half in range(2):
                    qh = jnp.where(halves[half], q, jnp.zeros_like(q))
                    scores = dot_t(qh, keys) + offset
                    before = top_ref[pair * 2 + half]
                    top = jnp.maximum(before, jnp.max(scores, axis=1, keepdims=True))
                    weights = jnp.exp2((scores - top) * factor).astype(BF16)
                    total = acc[pair * 2 + half] * jnp.exp2((before - top) * factor)
                    results.append((pair * 2 + half, weights, total))
            for index, weights, total in results:
                probs[index] = weights
                acc[index] = total
            return carry

        lax.fori_loop(0, pairs // 2, update, 0)

    def add_last(event):
        landed(1, event)

        def update(step, carry):
            results = []
            for pair in (step * 2, step * 2 + 1):
                values = recv_v[event, :, pair_span(pair)]
                for half in range(2):
                    total = acc[pair * 2 + half] + jnp.dot(
                        probs[pair * 2 + half],
                        jnp.where(halves[half], values, jnp.ones_like(values)),
                        preferred_element_type=F32,
                    )
                    results.append((pair * 2 + half, total))
            for index, total in results:
                acc[index] = total
            return carry

        lax.fori_loop(0, pairs // 2, update, 0)

    def absorb_event(way, hop):
        @pl.when(arrives(way, hop))
        def _():
            absorb(event_of(way, hop), source_plane(way, hop))

    absorb(0, plane)
    for hop in range(1, hops):
        for way in range(2):
            handle(way, hop + 1, (0, 1) if hop + 1 < hops else (0,))
        for way in range(2):
            absorb_event(way, hop)
    for way in range(2):

        @pl.when(arrives(way, hops))
        def _():
            weigh_last(event_of(way, hops), source_plane(way, hops))

        handle(way, hops, (1,))

        @pl.when(arrives(way, hops))
        def _():
            add_last(event_of(way, hops))

    def finish(tile):
        for pair in range(pairs):
            sums = [acc[pair * 2 + half, tile_span(tile), :] for half in range(2)]
            above = jnp.where(halves[0], sums[0], sums[1])
            below = pltpu.roll(jnp.where(halves[0], sums[1], sums[0]), HD, 1)
            att[tile_span(tile), pair * 2 * HD : (pair + 1) * 2 * HD] = (above / below).astype(
                BF16
            )

    def swap(tile):
        return pltpu.make_async_remote_copy(
            src_ref=part.at[tile],
            dst_ref=other.at[tile],
            send_sem=pair_send.at[tile],
            recv_sem=pair_recv.at[tile],
            device_id={"head": 1 - head},
            device_id_type=MESH,
        )

    for tile in range(tiles):
        finish(tile)
        part[tile] = jnp.dot(
            att[tile * DOCLEN : (tile + 1) * DOCLEN, :], ow_ref[...], preferred_element_type=F32
        ).astype(BF16)
        swap(tile).start()

    seg_row = jnp.zeros(seg_ref.shape, F32)
    here = pl.ds(pl.multiple_of(head * (model // 2), model // 2), model // 2)
    for tile in range(tiles):
        span = slice(tile * DOCLEN, (tile + 1) * DOCLEN)
        swap(tile).wait_recv()
        total = (
            x_ref[span, :].astype(F32) + part[tile].astype(F32) + other[tile].astype(F32)
        )
        mean = jnp.mean(total, axis=1, keepdims=True)
        centred = total - mean
        spread = jnp.mean(centred * centred, axis=1, keepdims=True)
        hidden[...] = centred * lax.rsqrt(spread + 1e-07)
        out_ref[span, :] = (
            hidden[:, here] * gain_ref[:, here] + lnb_ref[:, here]
        ).astype(BF16)
        firsts = jnp.concatenate(
            [hidden[row : row + 1, :] for row in range(0, DOCLEN, SHORT)], axis=0
        )
        full = firsts * gain_ref[...] + lnb_ref[...]
        scores = jnp.sum(full * sw_ref[...], axis=1, keepdims=True)
        segments = DOCLEN // SHORT
        lane_id = iota((segments, tiles * segments), 1) - tile * segments
        spread_scores = jnp.where(iota((segments, tiles * segments), 0) == lane_id, scores, 0.0)
        seg_row = seg_row + jnp.sum(spread_scores, axis=0, keepdims=True)
    seg_ref[...] = seg_row

    def drain(event):
        for which in range(2):
            lax.fori_loop(
                1, width, lambda step, carry: (deal(which, event, step).wait_send(), carry)[1], 0
            )

    drain(0)
    for way in range(2):
        for hop in range(1, hops + 1):

            @pl.when(departs(way, hop))
            def _():
                for which in range(2):
                    line(which, way, hop).wait_send()

            @pl.when(arrives(way, hop))
            def _():
                drain(event_of(way, hop))

    for tile in range(tiles):
        swap(tile).wait_send()


def shards(
    n,
    doc_x,
    doc_query,
    doc_key,
    doc_value,
    key_cache,
    value_cache,
    rel_embed,
    w_query,
    w_key,
    out_weight,
    ln_gain,
    ln_bias,
    score_weight,
    query_len,
    dev_query,
    page_table,
    tile_kind,
    rel_bucket,
):
    pages_here, page, cols = key_cache.shape
    queries, query_pages = page_table.shape
    tokens = query_pages * page
    block = pages_here // queries * page
    rows, model = doc_x.shape
    width = n // PLANES
    events = 2 * PLANES - 1
    tiles = rows // DOCLEN
    heads_here = cols // HD

    vmem = pl.BlockSpec(memory_space=pltpu.VMEM)
    smem = pl.BlockSpec(memory_space=pltpu.SMEM)
    normed, seg = pl.pallas_call(
        functools.partial(kernel, n),
        out_shape=(
            jax.ShapeDtypeStruct((rows, model // 2), BF16),
            jax.ShapeDtypeStruct((1, rows // SHORT), F32),
        ),
        in_specs=[smem] * 3 + [vmem] * 7 + [pl.BlockSpec(memory_space=pl.ANY)] * 8,
        out_specs=(vmem, vmem),
        scratch_shapes=[
            pltpu.VMEM(rel_embed.shape, BF16),
            pltpu.VMEM(w_key.shape, BF16),
            pltpu.VMEM(w_query.shape, BF16),
            pltpu.VMEM((rows, cols), BF16),
            pltpu.VMEM((rows, cols), BF16),
            pltpu.VMEM((rows, cols), BF16),
            pltpu.VMEM(out_weight.shape, BF16),
            pltpu.VMEM((rows, model), BF16),
            pltpu.VMEM((queries, block, cols), BF16),
            pltpu.VMEM((queries, block, cols), BF16),
            pltpu.VMEM((events * width, block, cols), BF16),
            pltpu.VMEM((events * width, block, cols), BF16),
            pltpu.VMEM((events, width * block, cols), BF16),
            pltpu.VMEM((events, width * block, cols), BF16),
            pltpu.VMEM((2 * DOCLEN, cols), BF16),
            pltpu.VMEM((2 * DOCLEN, cols), BF16),
            pltpu.VMEM((PLANES, 1, tokens // PLANES), F32),
            pltpu.VMEM((heads_here, rows, 1), F32),
            pltpu.VMEM((heads_here, rows, 2 * HD), F32),
            pltpu.VMEM((heads_here, rows, tokens // PLANES), BF16),
            pltpu.VMEM((rows, cols), BF16),
            pltpu.VMEM((tiles, DOCLEN, model), BF16),
            pltpu.VMEM((tiles, DOCLEN, model), BF16),
            pltpu.VMEM((DOCLEN, model), F32),
            pltpu.SemaphoreType.DMA((8,)),
            pltpu.SemaphoreType.DMA((2, 2, PLANES - 1)),
            pltpu.SemaphoreType.DMA((2, 2, PLANES - 1)),
            pltpu.SemaphoreType.DMA((2, events * width)),
            pltpu.SemaphoreType.DMA((2, events * width)),
            pltpu.SemaphoreType.DMA((tiles,)),
            pltpu.SemaphoreType.DMA((tiles,)),
        ]
        + [pltpu.VMEM((queries, block, cols), BF16)] * (4 * (PLANES - 1)),
        compiler_params=pltpu.CompilerParams(
            collective_id=0, has_side_effects=True, vmem_limit_bytes=56 * 1024 * 1024
        ),
        cost_estimate=pl.CostEstimate(
            flops=8_000_000_000, bytes_accessed=12_000_000, transcendentals=5_000_000
        ),
    )(
        tile_kind,
        dev_query,
        query_len,
        page_table,
        key_cache,
        value_cache,
        rel_bucket[None, :],
        ln_gain[None, :],
        ln_bias[None, :],
        score_weight[None, :],
        rel_embed,
        w_key,
        w_query,
        doc_query,
        doc_key,
        doc_value,
        out_weight,
        doc_x,
    )
    return normed, seg.reshape(-1)


def solution(mesh):
    in_specs = (
        P("blk", None),
        P("blk", "head"),
        P("blk", "head"),
        P("blk", "head"),
        P("blk", None, "head"),
        P("blk", None, "head"),
        P(),
        P(None, "head"),
        P(None, "head"),
        P("head", None),
        P(),
        P(),
        P(),
        P(),
        P(),
        P(),
        P("blk"),
        P(),
    )
    out_specs = (P("blk", "head"), P("blk"))
    return jax.shard_map(
        functools.partial(shards, mesh.shape["blk"]),
        mesh=mesh,
        in_specs=in_specs,
        out_specs=out_specs,
        check_vma=False,
    )
```
